512 devices in a mesh: cluster: 16 (over z), sub: 32 (over y, x, core).
Axes of the slice: x: 4, y: 4, z: 16, core: 2. Of those that a mesh axis runs over, the one named last changes fastest.
Arguments:
- features: bfloat16 [196608, 256], P(('cluster', 'sub')), may hold values from -6 to 6
- grad_out: bfloat16 [196608, 256], P(('cluster', 'sub')), may hold values from -6 to 6
- w_self: bfloat16 [256, 256], replicated, may hold values from -0.375 to 0.375
- w_neigh: bfloat16 [256, 256], replicated, may hold values from -0.375 to 0.375
- bias: float32 [256], replicated, may hold values from -3 to 3
- tile_dst: int32 [30720], P(('cluster', 'sub')), may hold values from 0 to 2
- tile_src: int32 [30720], P(('cluster', 'sub')), may hold values from 0 to 50, as said below
- tile_weight: bfloat16 [30720, 128, 128], P(('cluster', 'sub')), may hold values from 0 to 4
- recv_sub: int32 [512, 32], P(('cluster', 'sub')), may hold values from 0 to 1
- recv_cluster: int32 [512, 16], P(('cluster', 'sub')), may hold values from 0 to 1
Outputs:
- grad_features: bfloat16 [196608, 256], P(('cluster', 'sub'))
The draws below stay inside these ranges and needn't reach their ends.
Inputs may be any that keep to these rules, and one draw needn't show every extreme that they name: `tile_src`: within one partition's 60 tiles, each of the source-table entries 3 to 50 is named by exactly one tile; the other tiles name own blocks.
All inputs are finite; a program needn't handle non-finite values.
Results may differ from the reference program's by a relative error of at most 0.005.
Values may be sent and summed in bfloat16 or wider, within the bound.
A program may use at most 64 MiB of HBM per device.

```python
import jax
import jax.numpy as jnp
from jax import lax

D = 256
BLK = 128
OWN_BLK = 3
LOCAL_TILES = 12
BND = 2
TILES = 60
NODES = 196608
N_CLUSTER = 16
N_SUB = 32
DEVICES = 512


def draw_tile_src(key, part):
    key = jax.random.fold_in(key, 11)
    keys = jax.random.split(key, DEVICES)

    def one_device(device_key):
        first_key, second_key = jax.random.split(device_key)
        local = jax.random.randint(first_key, (LOCAL_TILES,), 0, OWN_BLK, dtype=jnp.int32)
        slots = OWN_BLK + jnp.arange(N_SUB + N_CLUSTER, dtype=jnp.int32)
        return jax.random.permutation(second_key, jnp.concatenate([slots, local])).astype(jnp.int32)
    return jax.vmap(one_device)(keys).reshape(-1)


def draw_tile_weight(key, part):
    key = jax.random.fold_in(key, 23)
    keys = jax.random.split(key, DEVICES * TILES)

    def one_tile(tile_key):
        order_key, heavy_key, extra_key = jax.random.split(tile_key, 3)
        order = jax.random.permutation(order_key, BLK).astype(jnp.int32)
        heavy = jax.random.randint(heavy_key, (BLK,), 2, 4, dtype=jnp.int32)
        extra = (jax.random.randint(extra_key, (BLK, BLK), 0, 64, dtype=jnp.int32) == 0).astype(jnp.int32)
        pattern = (order[:, None] == jnp.arange(BLK, dtype=jnp.int32)[None, :]).astype(jnp.int32)
        return (extra + pattern * heavy[:, None]).astype(jnp.float32)
    return jax.vmap(one_tile)(keys).astype(jnp.bfloat16)


def with_ends(values, stream_key, least, top_value):
    spot = [jax.random.randint(jax.random.fold_in(stream_key, axis), (), 0, length) for axis, length in enumerate(values.shape)]
    longest = values.shape.index(max(values.shape))
    neighbour = spot[:longest] + [(spot[longest] + 1) % values.shape[longest]] + spot[longest + 1:]
    return values.at[tuple(spot)].set(least).at[tuple(neighbour)].set(top_value)


def shard_levels(rng, shape, shards, least, largest):
    gain, own = 1.0, jax.random.fold_in(rng, 6)
    for dim, shards_of in shards:
        steps = jnp.exp(jax.random.uniform(jax.random.fold_in(own, dim), (shards_of,), jnp.float32, least / len(shards), largest / len(shards)))
        gain = gain * jnp.repeat(steps, shape[dim] // shards_of).reshape([-1 if axis == dim else 1 for axis in range(len(shape))])
    return gain


def gaussian(rng, dims, scale, reach, pieces=(), kind=jnp.bfloat16):
    array = scale * jax.random.normal(rng, dims, jnp.float32)
    if pieces:
        array = array * shard_levels(rng, dims, pieces, -0.22, 0.18)
    return jnp.clip(array, -reach, reach).astype(kind)


def setup_inputs(seed: int = 0) -> dict:
    key_list = jax.random.split(jax.random.key(seed), 11)
    features = gaussian(key_list[0], (NODES, D), 1.0, 6.0, ((0, 512),))
    grad_out = gaussian(key_list[1], (NODES, D), 1.0, 6.0, ((0, 512),))
    w_self = gaussian(key_list[2], (D, D), D ** -0.5, 0.375)
    w_neigh = gaussian(key_list[3], (D, D), D ** -0.5, 0.375)
    bias = gaussian(key_list[4], (D,), 0.5, 3.0, (), jnp.float32)
    tile_dst = with_ends(jax.random.randint(key_list[5], (N_CLUSTER * N_SUB * TILES,), 0, OWN_BLK), jax.random.fold_in(key_list[5], 1), 0, OWN_BLK - 1).astype(jnp.int32)
    tile_src = draw_tile_src(jax.random.fold_in(key_list[10], 71), 0)
    tile_weight = draw_tile_weight(jax.random.fold_in(key_list[10], 71), 0)
    recv_sub = with_ends(jax.random.randint(key_list[8], (N_CLUSTER * N_SUB, N_SUB), 0, BND), jax.random.fold_in(key_list[8], 1), 0, BND - 1).astype(jnp.int32)
    recv_cluster = with_ends(jax.random.randint(key_list[9], (N_CLUSTER * N_SUB, N_CLUSTER), 0, BND), jax.random.fold_in(key_list[9], 1), 0, BND - 1).astype(jnp.int32)
    return dict(features=features, grad_out=grad_out, w_self=w_self, w_neigh=w_neigh, bias=bias, tile_dst=tile_dst, tile_src=tile_src, tile_weight=tile_weight, recv_sub=recv_sub, recv_cluster=recv_cluster)


def gelu_tanh(values):
    return 0.5 * values * (1.0 + jnp.tanh(0.7978845608028654 * (values + 0.044715 * values * values * values)))

def reference(features, grad_out, w_self, w_neigh, bias, tile_dst, tile_src, tile_weight, recv_sub, recv_cluster):
    device_count = N_CLUSTER * N_SUB
    source_count = OWN_BLK + N_SUB + N_CLUSTER
    blocks = features.reshape(device_count, OWN_BLK, BLK, D)
    upstream = grad_out.reshape(device_count, OWN_BLK * BLK, D)
    dst_all = tile_dst.reshape(device_count, TILES)
    src_all = tile_src.reshape(device_count, TILES)
    weight_all = tile_weight.reshape(device_count, TILES, BLK, BLK)

    def step(carry, device):
        cluster_id = device // N_SUB
        sub_id = device % N_SUB
        sub_peers = cluster_id * N_SUB + jnp.arange(N_SUB, dtype=jnp.int32)
        cluster_peers = jnp.arange(N_CLUSTER, dtype=jnp.int32) * N_SUB + sub_id
        halo_sub = blocks[sub_peers, recv_sub[device]]
        halo_cluster = blocks[cluster_peers, recv_cluster[device]]
        source = jnp.concatenate([blocks[device], halo_sub, halo_cluster], axis=0)
        counts = weight_all[device].astype(jnp.float32)
        dst_ids = dst_all[device]
        src_ids = src_all[device]
        picked = source[src_ids].astype(jnp.float32)
        products = jnp.einsum('tij,tjd->tid', counts, picked, precision=lax.Precision.HIGHEST)
        aggregate = jnp.zeros((OWN_BLK, BLK, D), jnp.float32).at[dst_ids].add(products)
        degree = jnp.zeros((OWN_BLK, BLK), jnp.float32).at[dst_ids].add(lax.optimization_barrier(jnp.sum(counts, axis=2)))
        inverse = 1.0 / (degree + 1.0)
        neighbour_mean = (aggregate * inverse[:, :, None]).astype(jnp.bfloat16).reshape(OWN_BLK * BLK, D)
        own_rows = blocks[device].reshape(OWN_BLK * BLK, D)
        pre = jnp.dot(own_rows, w_self, preferred_element_type=jnp.float32)
        pre = pre + jnp.dot(neighbour_mean, w_neigh, preferred_element_type=jnp.float32) + bias
        _, pullback = jax.vjp(gelu_tanh, pre)
        grad_pre = pullback(upstream[device].astype(jnp.float32))[0].astype(jnp.bfloat16)
        grad_self = jnp.dot(grad_pre, w_self.T, preferred_element_type=jnp.float32)
        spread = jnp.dot(grad_pre, w_neigh.T, preferred_element_type=jnp.float32).reshape(OWN_BLK, BLK, D)
        spread = (spread * inverse[:, :, None]).astype(jnp.bfloat16)
        returned = jnp.einsum('tij,tid->tjd', counts, spread[dst_ids].astype(jnp.float32), precision=lax.Precision.HIGHEST)
        partial_value = jnp.zeros((source_count, BLK, D), jnp.float32).at[src_ids].add(returned)
        remote = lax.optimization_barrier(partial_value[OWN_BLK:].astype(jnp.bfloat16)).astype(jnp.float32)
        carry = carry.at[device].add(partial_value[:OWN_BLK])
        carry = carry.at[sub_peers, recv_sub[device]].add(remote[:N_SUB])
        carry = carry.at[cluster_peers, recv_cluster[device]].add(remote[N_SUB:])
        return (carry, grad_self)
    start = jnp.zeros((device_count, OWN_BLK, BLK, D), jnp.float32)
    back, grad_self = lax.scan(step, start, jnp.arange(device_count, dtype=jnp.int32))
    total = grad_self.reshape(NODES, D) + back.reshape(NODES, D)
    return total.astype(jnp.bfloat16)
```

```python
import functools

import jax
import jax.numpy as jnp
from jax import lax
from jax.experimental import pallas as pl
from jax.experimental.pallas import tpu as pltpu
from jax.sharding import PartitionSpec as P

MESH = pl.DeviceIdType.MESH
BF = jnp.bfloat16
F32 = jnp.float32
NZ = 16
RING = 4
HALF = NZ // 2
BLK = 128
D = 256
OWN = 3
TILES = 60
N_SUB = 32
REMOTE = N_SUB + NZ
LOCAL = TILES - REMOTE


def wrap(value, size):
    return lax.rem(value + size, size)


def dot_nt(left, right):
    return lax.dot_general(left, right, (((1,), (1,)), ((), ())), preferred_element_type=F32)


def kernel(
    src_ref, dst_ref, rsub_ref, rclu_ref,
    feat, gout, ws, wn, bias, tiles_hbm,
    out,
    w, wt, tab, acc, deg, pre, inv, spread, gself,
    zu, zd, gs, gb,
    pu, pd, su, sd, ru, rd,
    sb, rb, sbp, sbh, rbp, rbh, sap, sah, rap, rah,
    w_sem,
    zu_s, zu_r, zd_s, zd_r, a_s, a_r, b_s, b_r, x_s, x_r,
    ku_s, ku_r, kd_s, kd_r, ka_s, ka_r, kb_s, kb_r, kx_s, kx_r,
):
    c = lax.axis_index("cluster")
    s = lax.axis_index("sub")
    core = lax.rem(s, 2)
    x = lax.rem(s // 2, RING)
    y = s // (2 * RING)
    a = x * (1 - core) + y * core
    b = y * (1 - core) + x * core

    def at(da, db, which):
        aa = wrap(a + da, RING)
        bb = wrap(b + db, RING)
        xx = aa * (1 - core) + bb * core
        yy = bb * (1 - core) + aa * core
        return (yy * RING + xx) * 2 + which

    up = (wrap(c + 1, NZ), s)
    dn = (wrap(c - 1, NZ), s)
    ap = (c, at(1, 0, core))
    am = (c, at(-1, 0, core))
    bp = (c, at(0, 1, core))
    bm = (c, at(0, -1, core))
    sib = (c, at(0, 0, 1 - core))

    def copy(source, target, send, recv, device):
        return pltpu.make_async_remote_copy(
            src_ref=source, dst_ref=target, send_sem=send, recv_sem=recv,
            device_id=device, device_id_type=MESH,
        )

    def same_index(da, db):
        return at(-da, -db, core)

    def other_index(da, db):
        return at(-db, -da, 1 - core)

    load = pltpu.make_async_copy(tiles_hbm, w, w_sem)
    load.start()
    barrier = pltpu.get_barrier_semaphore()
    for device in (up, dn, ap, am, bp, bm, sib):
        pl.semaphore_signal(barrier, inc=1, device_id=device, device_id_type=MESH)
    gs[0, 0] = feat[0:2]
    acc[...] = jnp.zeros_like(acc)
    deg[...] = jnp.zeros_like(deg)
    pl.semaphore_wait(barrier, 7)

    def zu_copy(d, h):
        source = feat.at[h] if d == 1 else zu.at[d - 2, h]
        return copy(source, zu.at[d - 1, h], zu_s.at[d - 1, h], zu_r.at[d - 1, h], up)

    def zd_copy(d, h):
        source = feat.at[h] if d == 1 else zd.at[d - 2, h]
        return copy(source, zd.at[d - 1, h], zd_s.at[d - 1, h], zd_r.at[d - 1, h], dn)

    def has_up(d, h):
        return d < HALF or (d == HALF and h == 0)

    def has_dn(d, h):
        return d < HALF or (d == HALF and h == 1)

    def a_copy(k):
        source, target, device = (
            (gs.at[0, 0], gs.at[1, 0], ap),
            (gs.at[0, 0], gs.at[3, 0], am),
            (gs.at[1, 0, 0], gs.at[2, 0, 0], ap),
            (gs.at[3, 0, 1], gs.at[2, 0, 1], am),
        )[k]
        return copy(source, target, a_s.at[k], a_r.at[k], device)

    def b_copy(da, k):
        source, target, device = (
            (gs.at[da, 0], gs.at[da, 1], bp),
            (gs.at[da, 0], gs.at[da, 3], bm),
            (gs.at[da, 1, 0], gs.at[da, 2, 0], bp),
            (gs.at[da, 3, 1], gs.at[da, 2, 1], bm),
        )[k]
        return copy(source, target, b_s.at[da, k], b_r.at[da, k], device)

    def x_copy(da, db):
        return copy(gs.at[da, db], gb.at[da, db], x_s.at[da, db], x_r.at[da, db], sib)

    def z_start():
        for h in (0, 1):
            zu_copy(1, h).start()
            zd_copy(1, 1 - h).start()

    def z_step(d, h):
        if has_up(d, h):
            zu_copy(d, h).wait_recv()
            if has_up(d + 1, h):
                zu_copy(d + 1, h).start()
        if has_dn(d, 1 - h):
            zd_copy(d, 1 - h).wait_recv()
            if has_dn(d + 1, 1 - h):
                zd_copy(d + 1, 1 - h).start()

    def a_start():
        a_copy(0).start()
        a_copy(1).start()

    def a_mid():
        a_copy(0).wait_recv()
        a_copy(2).start()
        a_copy(1).wait_recv()
        a_copy(3).start()
        for da in (1, 3):
            b_start(da)
            x_copy(da, 0).start()

    def a_end():
        a_copy(2).wait_recv()
        a_copy(3).wait_recv()
        b_start(2)
        x_copy(2, 0).start()

    def b_start(da):
        b_copy(da, 0).start()
        b_copy(da, 1).start()

    def b_mid(da):
        b_copy(da, 0).wait_recv()
        b_copy(da, 2).start()
        b_copy(da, 1).wait_recv()
        b_copy(da, 3).start()
        x_copy(da, 1).start()
        x_copy(da, 3).start()

    def b_end(da):
        b_copy(da, 2).wait_recv()
        b_copy(da, 3).wait_recv()
        x_copy(da, 2).start()

    def find_remote(first, count):
        def body(i, _):
            terms = [jnp.where(src_ref[t] == i + OWN, t, 0) for t in range(TILES)]
            while len(terms) > 1:
                terms = [sum(terms[k : k + 2]) for k in range(0, len(terms), 2)]
            tab[i] = terms[0]
            return 0

        lax.fori_loop(first, first + count, body, 0)

    def find_local():
        def body(t, carry):
            seen, found = carry
            local = src_ref[t] < OWN
            found = tuple(
                jnp.where(jnp.logical_and(local, seen == k), t, found[k]) for k in range(LOCAL)
            )
            return seen + jnp.where(local, 1, 0), found

        zero = jnp.int32(0)
        _, found = lax.fori_loop(0, TILES, body, (zero, (zero,) * LOCAL))
        for k in range(LOCAL):
            tab[REMOTE + k] = found[k]

    def transpose_tiles(first, count):
        def body(t, _):
            wt[t] = w[t].T
            return 0

        lax.fori_loop(first, first + count, body, 0)

    def accumulate(i0, block0, i1, block1):
        rows = []
        t0, t1 = tab[i0], tab[i1]
        w0, w1 = w[t0], w[t1]
        d0, d1 = dst_ref[t0], dst_ref[t1]
        zero = jnp.zeros((BLK, BLK), BF)
        for k in range(OWN):
            rows.append(
                jnp.concatenate([jnp.where(d0 == k, w0, zero), jnp.where(d1 == k, w1, zero)], axis=1)
            )
        left = jnp.concatenate(rows, axis=0)
        right = jnp.concatenate([block0, block1], axis=0)
        acc[...] += jnp.dot(left, right, preferred_element_type=F32)
        deg[...] += jnp.dot(left, jnp.ones((2 * BLK, BLK), BF), preferred_element_type=F32)

    def z_pair(d):
        r0, r1 = wrap(c - d, NZ), wrap(c + d, NZ)
        block0 = jnp.where(rclu_ref[0, r0] == 0, zu[d - 1, 0], zu[d - 1, 1])
        block1 = jnp.where(rclu_ref[0, r1] == 0, zd[d - 1, 0], zd[d - 1, 1])
        accumulate(N_SUB + r0, block0, N_SUB + r1, block1)

    def z_last():
        r0 = wrap(c + HALF, NZ)
        block0 = jnp.where(rclu_ref[0, r0] == 0, zu[HALF - 1, 0], zd[HALF - 1, 1])
        block1 = jnp.where(rclu_ref[0, c] == 0, feat[0], feat[1])
        accumulate(N_SUB + r0, block0, N_SUB + c, block1)

    def sub_pairs(da):
        def body(db, _):
            x_copy(da, db).wait_recv()
            p0, p1 = same_index(da, db), other_index(da, db)
            block0 = jnp.where(rsub_ref[0, p0] == 0, gs[da, db, 0], gs[da, db, 1])
            block1 = jnp.where(rsub_ref[0, p1] == 0, gb[da, db, 0], gb[da, db, 1])
            accumulate(p0, block0, p1, block1)
            return 0

        lax.fori_loop(0, RING, body, 0)

    def local_pairs():
        def body(k, _):
            i0 = REMOTE + 2 * k
            i1 = i0 + 1
            accumulate(i0, feat[src_ref[tab[i0]]], i1, feat[src_ref[tab[i1]]])
            return 0

        lax.fori_loop(0, LOCAL // 2, body, 0)

    def self_product():
        rows = feat[...].reshape(OWN * BLK, D)
        pre[...] = jnp.dot(rows, ws[...], preferred_element_type=F32) + bias[...]

    z_start()
    a_start()
    b_start(0)
    x_copy(0, 0).start()
    self_product()
    load.wait()
    find_local()

    z_step(1, 0)
    find_remote(N_SUB, NZ // 2)
    z_step(1, 1)
    a_mid()
    b_mid(0)
    find_remote(N_SUB + NZ // 2, NZ // 2)

    z_step(2, 0)
    z_pair(1)
    z_step(2, 1)
    a_end()
    b_mid(1)
    b_mid(3)
    b_end(0)
    find_remote(0, 8)

    z_step(3, 0)
    z_pair(2)
    find_remote(8, 8)
    z_step(3, 1)
    b_mid(2)
    b_end(1)
    b_end(3)
    find_remote(16, 8)

    z_step(4, 0)
    z_pair(3)
    find_remote(24, 8)
    z_step(4, 1)
    b_end(2)
    transpose_tiles(0, 20)

    z_step(5, 0)
    z_pair(4)
    transpose_tiles(20, 20)
    z_step(5, 1)
    sub_pairs(0)

    z_step(6, 0)
    z_pair(5)
    transpose_tiles(40, 20)
    z_step(6, 1)
    sub_pairs(1)

    z_step(7, 0)
    z_pair(6)
    sub_pairs(3)
    z_step(7, 1)
    z_pair(7)
    sub_pairs(2)
    local_pairs()
    z_step(8, 0)
    z_last()

    scale = 1.0 / (deg[...] + 1.0)
    inv[...] = jnp.concatenate([scale, scale], axis=1)
    mean = (acc[...] * inv[...]).astype(BF)
    v = pre[...] + jnp.dot(mean, wn[...], preferred_element_type=F32)
    k0, k1 = 0.7978845608028654, 0.044715
    square = v * v
    th = jnp.tanh(k0 * v * (1.0 + k1 * square))
    slope = 0.5 * (1.0 + th) + 0.5 * v * (1.0 - th * th) * (k0 * (1.0 + 3.0 * k1 * square))
    grad_pre = (gout[...].astype(F32) * slope).astype(BF)
    spread[...] = (dot_nt(grad_pre, wn[...]) * inv[...]).astype(BF).reshape(OWN, BLK, D)

    def partial(i):
        t = tab[i]
        return jnp.dot(wt[t], spread[dst_ref[t]], preferred_element_type=F32)

    def only(keep, value):
        return jnp.where(keep, value, jnp.zeros_like(value))

    def ku_copy(d, h):
        return copy(su.at[d - 1, h], ru.at[d - 1, h], ku_s.at[d - 1, h], ku_r.at[d - 1, h], up)

    def kd_copy(d, h):
        return copy(sd.at[d - 1, h], rd.at[d - 1, h], kd_s.at[d - 1, h], kd_r.at[d - 1, h], dn)

    def ku_send(d, h):
        value = only(rclu_ref[0, wrap(c + d, NZ)] == h, pu[d - 1])
        if has_up(d + 1, h):
            ku_copy(d + 1, h).wait_recv()
            value = value + ru[d, h].astype(F32)
        su[d - 1, h] = value.astype(BF)
        ku_copy(d, h).start()

    def kd_send(d, h):
        value = only(rclu_ref[0, wrap(c - d, NZ)] == h, pd[d - 1])
        if has_dn(d + 1, h):
            kd_copy(d + 1, h).wait_recv()
            value = value + rd[d, h].astype(F32)
        sd[d - 1, h] = value.astype(BF)
        kd_copy(d, h).start()

    def z_partials(d):
        pu[d - 1] = partial(N_SUB + wrap(c + d, NZ))
        pd[d - 1] = partial(N_SUB + wrap(c - d, NZ))

    def kx_copy(da, db):
        return copy(sb.at[da, db], rb.at[da, db], kx_s.at[da, db], kx_r.at[da, db], sib)

    def x_send(da):
        def body(db, _):
            p = other_index(da, db)
            value = partial(p)
            for h in (0, 1):
                sb[da, db, h] = only(rsub_ref[0, p] == h, value).astype(BF)
            kx_copy(da, db).start()
            return 0

        lax.fori_loop(0, RING, body, 0)

    def kb_copy(da, k):
        source, target, device = (
            (sbp.at[da, 0], rbp.at[da, 0], bm),
            (sbp.at[da, 1], rbp.at[da, 1], bp),
            (sbh.at[da, 0], rbh.at[da, 0], bm),
            (sbh.at[da, 1], rbh.at[da, 1], bp),
        )[k]
        return copy(source, target, kb_s.at[da, k], kb_r.at[da, k], device)

    def ka_copy(k):
        source, target, device = (
            (sap.at[0], rap.at[0], am),
            (sap.at[1], rap.at[1], ap),
            (sah.at[0], rah.at[0], am),
            (sah.at[1], rah.at[1], ap),
        )[k]
        return copy(source, target, ka_s.at[k], ka_r.at[k], device)

    def chip_sum(da, db):
        p = same_index(da, db)
        value = partial(p)
        kx_copy(da, db).wait_recv()
        return [
            only(rsub_ref[0, p] == h, value) + rb[da, db, h].astype(F32) for h in (0, 1)
        ]

    def b_far(da):
        v0, v1 = chip_sum(da, 2)
        sbh[da, 0] = v0.astype(BF)
        kb_copy(da, 2).start()
        sbh[da, 1] = v1.astype(BF)
        kb_copy(da, 3).start()

    def b_near(da):
        v0, v1 = chip_sum(da, 1)
        sbp[da, 0, 1] = v1.astype(BF)
        kb_copy(da, 2).wait_recv()
        sbp[da, 0, 0] = (v0 + rbh[da, 0].astype(F32)).astype(BF)
        kb_copy(da, 0).start()
        v0, v1 = chip_sum(da, 3)
        sbp[da, 1, 0] = v0.astype(BF)
        kb_copy(da, 3).wait_recv()
        sbp[da, 1, 1] = (v1 + rbh[da, 1].astype(F32)).astype(BF)
        kb_copy(da, 1).start()

    def row_sum(da):
        v = chip_sum(da, 0)
        kb_copy(da, 0).wait_recv()
        kb_copy(da, 1).wait_recv()
        return [v[h] + rbp[da, 0, h].astype(F32) + rbp[da, 1, h].astype(F32) for h in (0, 1)]

    def a_far():
        v = row_sum(2)
        sah[0] = v[0].astype(BF)
        ka_copy(2).start()
        sah[1] = v[1].astype(BF)
        ka_copy(3).start()

    def a_near():
        v = row_sum(1)
        ka_copy(2).wait_recv()
        sap[0, 0] = (v[0] + rah[0].astype(F32)).astype(BF)
        sap[0, 1] = v[1].astype(BF)
        ka_copy(0).start()
        v = row_sum(3)
        ka_copy(3).wait_recv()
        sap[1, 0] = v[0].astype(BF)
        sap[1, 1] = (v[1] + rah[1].astype(F32)).astype(BF)
        ka_copy(1).start()

    def add_local():
        def body(k, _):
            i = REMOTE + k
            value = partial(i)
            j = src_ref[tab[i]]
            for n in range(OWN):
                gself[n] += only(j == n, value)
            return 0

        lax.fori_loop(0, LOCAL, body, 0)
        value = partial(N_SUB + c)
        for h in (0, 1):
            gself[h] += only(rclu_ref[0, c] == h, value)

    z_partials(HALF)
    su[HALF - 1, 0] = only(rclu_ref[0, wrap(c + HALF, NZ)] == 0, pu[HALF - 1]).astype(BF)
    ku_copy(HALF, 0).start()
    sd[HALF - 1, 1] = only(rclu_ref[0, wrap(c + HALF, NZ)] == 1, pd[HALF - 1]).astype(BF)
    kd_copy(HALF, 1).start()
    z_partials(7)
    ku_send(7, 1)
    kd_send(7, 0)
    gself[...] = dot_nt(grad_pre, ws[...]).reshape(OWN, BLK, D)
    x_send(2)
    z_partials(6)

    ku_send(7, 0)
    kd_send(7, 1)
    x_send(1)
    ku_send(6, 1)
    kd_send(6, 0)
    x_send(3)
    z_partials(5)

    ku_send(6, 0)
    kd_send(6, 1)
    b_far(2)
    ku_send(5, 1)
    kd_send(5, 0)
    x_send(0)
    z_partials(4)

    ku_send(5, 0)
    kd_send(5, 1)
    b_far(1)
    b_far(3)
    ku_send(4, 1)
    kd_send(4, 0)
    b_far(0)
    z_partials(3)

    ku_send(4, 0)
    kd_send(4, 1)
    b_near(2)
    ku_send(3, 1)
    kd_send(3, 0)
    b_near(1)
    z_partials(2)

    ku_send(3, 0)
    kd_send(3, 1)
    b_near(3)
    ku_send(2, 1)
    kd_send(2, 0)
    b_near(0)
    z_partials(1)

    ku_send(2, 0)
    kd_send(2, 1)
    a_far()
    ku_send(1, 1)
    kd_send(1, 0)
    a_near()
    ku_send(1, 0)
    kd_send(1, 1)
    add_local()

    v = row_sum(0)
    ka_copy(0).wait_recv()
    ka_copy(1).wait_recv()
    out[2] = gself[2].astype(BF)
    for h in (0, 1):
        ku_copy(1, h).wait_recv()
        kd_copy(1, h).wait_recv()
        total = gself[h] + v[h] + rap[0, h].astype(F32) + rap[1, h].astype(F32)
        total = total + ru[0, h].astype(F32) + rd[0, h].astype(F32)
        out[h] = total.astype(BF)

    for d in range(1, HALF + 1):
        for h in (0, 1):
            if has_up(d, h):
                zu_copy(d, h).wait_send()
                ku_copy(d, h).wait_send()
            if has_dn(d, h):
                zd_copy(d, h).wait_send()
                kd_copy(d, h).wait_send()
    for k in range(4):
        a_copy(k).wait_send()
        ka_copy(k).wait_send()
    for da in range(RING):
        for k in range(4):
            b_copy(da, k).wait_send()
            kb_copy(da, k).wait_send()
        for db in range(RING):
            x_copy(da, db).wait_send()
            kx_copy(da, db).wait_send()


def shards(
    features, grad_out, w_self, w_neigh, bias, tile_dst, tile_src, tile_weight, recv_sub, recv_cluster
):
    blk = (BLK, D)
    smem = pl.BlockSpec(memory_space=pltpu.SMEM)
    vmem = pl.BlockSpec(memory_space=pltpu.VMEM)
    sems = [(HALF, 2)] * 4 + [(4,)] * 2 + [(RING, 4)] * 2 + [(RING, RING)] * 2
    scratch = [
        pltpu.VMEM((TILES, BLK, BLK), BF),
        pltpu.VMEM((TILES, BLK, BLK), BF),
        pltpu.SMEM((TILES,), jnp.int32),
        pltpu.VMEM((OWN * BLK, D), F32),
        pltpu.VMEM((OWN * BLK, BLK), F32),
        pltpu.VMEM((OWN * BLK, D), F32),
        pltpu.VMEM((OWN * BLK, D), F32),
        pltpu.VMEM((OWN,) + blk, BF),
        pltpu.VMEM((OWN,) + blk, F32),
        pltpu.VMEM((HALF, 2) + blk, BF),
        pltpu.VMEM((HALF, 2) + blk, BF),
        pltpu.VMEM((RING, RING, 2) + blk, BF),
        pltpu.VMEM((RING, RING, 2) + blk, BF),
        pltpu.VMEM((HALF,) + blk, F32),
        pltpu.VMEM((HALF,) + blk, F32),
        pltpu.VMEM((HALF, 2) + blk, BF),
        pltpu.VMEM((HALF, 2) + blk, BF),
        pltpu.VMEM((HALF, 2) + blk, BF),
        pltpu.VMEM((HALF, 2) + blk, BF),
        pltpu.VMEM((RING, RING, 2) + blk, BF),
        pltpu.VMEM((RING, RING, 2) + blk, BF),
        pltpu.VMEM((RING, 2, 2) + blk, BF),
        pltpu.VMEM((RING, 2) + blk, BF),
        pltpu.VMEM((RING, 2, 2) + blk, BF),
        pltpu.VMEM((RING, 2) + blk, BF),
        pltpu.VMEM((2, 2) + blk, BF),
        pltpu.VMEM((2,) + blk, BF),
        pltpu.VMEM((2, 2) + blk, BF),
        pltpu.VMEM((2,) + blk, BF),
        pltpu.SemaphoreType.DMA,
    ] + [pltpu.SemaphoreType.DMA(shape) for shape in sems + sems]
    result = pl.pallas_call(
        kernel,
        out_shape=jax.ShapeDtypeStruct((OWN,) + blk, BF),
        in_specs=[smem] * 4 + [vmem] * 5 + [pl.BlockSpec(memory_space=pl.ANY)],
        out_specs=vmem,
        scratch_shapes=scratch,
        compiler_params=pltpu.CompilerParams(
            collective_id=0, has_side_effects=True, vmem_limit_bytes=48 * 1024 * 1024
        ),
        name="sage_layer",
    )(
        tile_src, tile_dst, recv_sub, recv_cluster,
        features.reshape((OWN,) + blk), grad_out, w_self, w_neigh, bias.reshape(1, D), tile_weight,
    )
    return result.reshape(OWN * BLK, D)


def solution(mesh):
    rows = P(("cluster", "sub"), None)
    flat = P(("cluster", "sub"))
    placed = (rows, rows, P(), P(), P(), flat, flat, P(("cluster", "sub"), None, None), rows, rows)
    return jax.shard_map(shards, mesh=mesh, in_specs=placed, out_specs=rows, check_vma=False)
```

```python
import functools

import jax
import jax.numpy as jnp
from jax import lax
from jax.experimental import pallas as pl
from jax.experimental.pallas import tpu as pltpu
from jax.sharding import PartitionSpec as P

MESH = pl.DeviceIdType.MESH
BF = jnp.bfloat16
F32 = jnp.float32
NZ = 16
RING = 4
HALF = NZ // 2
BLK = 128
D = 256
OWN = 3
TILES = 60
N_SUB = 32
REMOTE = N_SUB + NZ
LOCAL = TILES - REMOTE
SLOTS = 128
SKIP_F = 0
SKIP_B = 0
CHUNKS = 4
PER = CHUNKS // 2
ROWS = BLK // PER
VMEM_BYTES = 62 * 1024 * 1024


def wrap(value, size):
    return lax.rem(value + size, size)


def dot_nt(left, right):
    return lax.dot_general(left, right, (((1,), (1,)), ((), ())), preferred_element_type=F32)


def kernel(
    src_hbm, dst_hbm, rsub_hbm, rclu_hbm,
    feat_hbm, gout_hbm, ws_hbm, wn_hbm, bias_hbm, tiles_hbm,
    out,
    src_ref, dst_ref, rsub_ref, rclu_ref, feat, gout, ws, wn, bias,
    src_row, tab_row, w, wt, tab, acc, deg, pre, inv, spread, gself,
    zu, zd, gs, gb,
    pu, pd, su, sd, ru, rd,
    sb, rb, sbp, sbh, rbp, rbh, sap, sah, rap, rah,
    in_s,
    zu_s, zu_r, zd_s, zd_r, a_s, a_r, b_s, b_r, x_s, x_r,
    ku_s, ku_r, kd_s, kd_r, ka_s, ka_r, kb_s, kb_r, kx_s, kx_r,
):
    c = lax.axis_index("cluster")
    s = lax.axis_index("sub")
    core = lax.rem(s, 2)
    x = lax.rem(s // 2, RING)
    y = s // (2 * RING)
    a = x * (1 - core) + y * core
    b = y * (1 - core) + x * core

    def at(da, db, which):
        aa = wrap(a + da, RING)
        bb = wrap(b + db, RING)
        xx = aa * (1 - core) + bb * core
        yy = bb * (1 - core) + aa * core
        return (yy * RING + xx) * 2 + which

    up = (wrap(c + 1, NZ), s)
    dn = (wrap(c - 1, NZ), s)
    up2 = (wrap(c + 2, NZ), s)
    dn2 = (wrap(c - 2, NZ), s)
    ap = (c, at(1, 0, core))
    am = (c, at(-1, 0, core))
    bp = (c, at(0, 1, core))
    bm = (c, at(0, -1, core))
    sib = (c, at(0, 0, 1 - core))

    def copy(source, target, send, recv, device):
        return pltpu.make_async_remote_copy(
            src_ref=source, dst_ref=target, send_sem=send, recv_sem=recv,
            device_id=device, device_id_type=MESH,
        )

    def same_index(da, db):
        return at(-da, -db, core)

    def other_index(da, db):
        return at(-db, -da, 1 - core)

    inputs = (
        (feat_hbm, feat), (src_hbm, src_ref), (src_hbm, src_row), (dst_hbm, dst_ref), (rsub_hbm, rsub_ref),
        (rclu_hbm, rclu_ref), (ws_hbm, ws), (bias_hbm, bias), (tiles_hbm, w), (wn_hbm, wn),
        (gout_hbm, gout),
    )
    loads = [pltpu.make_async_copy(*pair, in_s.at[k]) for k, pair in enumerate(inputs)]
    for load in loads:
        load.start()
    barrier = pltpu.get_barrier_semaphore()
    for device in (up, dn, up2, dn2, ap, am, bp, bm, sib):
        pl.semaphore_signal(barrier, inc=1, device_id=device, device_id_type=MESH)
    pl.semaphore_wait(barrier, 9)

    def rows_of(q):
        return q // PER, pl.ds(q % PER * ROWS, ROWS)

    def is_far(up_way, q):
        return (q < PER) == up_way

    def has(up_way, d, q):
        return d < HALF or (d == HALF and is_far(up_way, q))

    def z_copy(up_way, d, q):
        buf, send, recv = (zu, zu_s, zu_r) if up_way else (zd, zd_s, zd_r)
        h, rows = rows_of(q)
        source = buf.at[d - 2, h, rows] if d > 1 else feat_hbm.at[h, rows]
        device = up if up_way else dn
        if SKIP_F and d == 2 and is_far(up_way, q):
            source = feat_hbm.at[h, rows]
            device = up2 if up_way else dn2
        return copy(source, buf.at[d - 1, h, rows], send.at[d - 1, q], recv.at[d - 1, q], device)

    def z_start():
        for d, far in ((1, False), (2, True), (1, True)) if SKIP_F else ((1, True), (1, False)):
            for q in range(CHUNKS):
                for up_way in (True, False):
                    if is_far(up_way, q) == far:
                        z_copy(up_way, d, q).start()

    def z_step(r, far):
        d = r + 1 if far else r
        if SKIP_F and d == 1 and far:
            return
        for q in range(PER):
            for up_way in (True, False):
                p = q if far == up_way else q + PER
                z_copy(up_way, d, p).wait_recv()
                if has(up_way, d + 1, p):
                    z_copy(up_way, d + 1, p).start()

    def z_first():
        if not SKIP_F:
            return
        for q in range(CHUNKS):
            for up_way in (True, False):
                if is_far(up_way, q):
                    z_copy(up_way, 1, q).wait_recv()

    own = feat_hbm.at[pl.ds(0, 2)]

    def a_copy(k):
        source, target, device = (
            (own, gs.at[1, 0], ap),
            (own, gs.at[3, 0], am),
            (gs.at[1, 0, 0], gs.at[2, 0, 0], ap),
            (gs.at[3, 0, 1], gs.at[2, 0, 1], am),
        )[k]
        return copy(source, target, a_s.at[k], a_r.at[k], device)

    def b_copy(da, k):
        source, target, device = (
            (gs.at[da, 0] if da else own, gs.at[da, 1], bp),
            (gs.at[da, 0] if da else own, gs.at[da, 3], bm),
            (gs.at[da, 1, 0], gs.at[da, 2, 0], bp),
            (gs.at[da, 3, 1], gs.at[da, 2, 1], bm),
        )[k]
        return copy(source, target, b_s.at[da, k], b_r.at[da, k], device)

    def x_copy(da, db):
        source = gs.at[da, db]
        if da == 0 and isinstance(db, int) and db == 0:
            source = own
        return copy(source, gb.at[da, db], x_s.at[da, db], x_r.at[da, db], sib)

    def a_start():
        a_copy(0).start()
        a_copy(1).start()

    def a_mid():
        a_copy(0).wait_recv()
        a_copy(2).start()
        a_copy(1).wait_recv()
        a_copy(3).start()
        for da in (1, 3):
            b_start(da)
            x_copy(da, 0).start()

    def a_end():
        a_copy(2).wait_recv()
        a_copy(3).wait_recv()
        b_start(2)
        x_copy(2, 0).start()

    def b_start(da):
        b_copy(da, 0).start()
        b_copy(da, 1).start()

    def b_mid(da):
        b_copy(da, 0).wait_recv()
        b_copy(da, 2).start()
        b_copy(da, 1).wait_recv()
        b_copy(da, 3).start()
        x_copy(da, 1).start()
        x_copy(da, 3).start()

    def b_end(da):
        b_copy(da, 2).wait_recv()
        b_copy(da, 3).wait_recv()
        x_copy(da, 2).start()

    def find_tiles():
        row = lax.broadcasted_iota(jnp.int32, (TILES, TILES), 0)
        col = lax.broadcasted_iota(jnp.int32, (TILES, TILES), 1)
        by_col = jnp.broadcast_to(src_row[...], (TILES, TILES))
        earlier = jnp.where(jnp.logical_and(by_col < OWN, col < row), 1, 0)
        earlier = jnp.sum(earlier, axis=1, keepdims=True)
        src = jnp.broadcast_to(src_row[...], (SLOTS, TILES)).T
        place = jnp.where(src < OWN, REMOTE + earlier, src - OWN)
        tile = lax.broadcasted_iota(jnp.int32, (TILES, SLOTS), 0)
        slot = lax.broadcasted_iota(jnp.int32, (TILES, SLOTS), 1)
        tab_row[...] = jnp.sum(jnp.where(place == slot, tile, 0), axis=0, keepdims=True)
        move = pltpu.make_async_copy(tab_row, tab, in_s.at[0])
        move.start()
        return move

    def transpose_tiles(first, count):
        def body(t, _):
            wt[t] = w[t].T
            return 0

        lax.fori_loop(first, first + count, body, 0)

    def tile_row(entries):
        tiles = [tab[0, i] for i in entries]
        zero = jnp.zeros((BLK, BLK), BF)
        return jnp.concatenate(
            [
                jnp.concatenate([jnp.where(dst_ref[0, t] == k, w[t], zero) for t in tiles], axis=1)
                for k in range(OWN)
            ],
            axis=0,
        )

    def accumulate(entries, blocks, count=True):
        left = tile_row(entries)
        acc[...] += jnp.dot(left, jnp.concatenate(blocks, axis=0), preferred_element_type=F32)
        if count:
            add_degree(left)

    def add_degree(left):
        ones = jnp.ones((left.shape[1], BLK), BF)
        deg[...] += jnp.dot(left, ones, preferred_element_type=F32)

    def invert_degree():
        late = [wrap(c - 7, NZ), wrap(c + 7, NZ), wrap(c + HALF, NZ), c]
        add_degree(tile_row([N_SUB + r for r in late]))
        scale = 1.0 / (deg[...] + 1.0)
        inv[...] = jnp.concatenate([scale, scale], axis=1)

    def z_pair(d):
        r0, r1 = wrap(c - d, NZ), wrap(c + d, NZ)
        block0 = jnp.where(rclu_ref[0, r0] == 0, zu[d - 1, 0], zu[d - 1, 1])
        block1 = jnp.where(rclu_ref[0, r1] == 0, zd[d - 1, 0], zd[d - 1, 1])
        accumulate([N_SUB + r0, N_SUB + r1], [block0, block1], d < 7)

    def z_last():
        r0 = wrap(c + HALF, NZ)
        block0 = jnp.where(rclu_ref[0, r0] == 0, zu[HALF - 1, 0], zd[HALF - 1, 1])
        block1 = jnp.where(rclu_ref[0, c] == 0, feat[0], feat[1])
        accumulate([N_SUB + r0, N_SUB + c], [block0, block1], False)

    def sub_pairs(da, first):
        entries, blocks = [], []
        for db in (first, first + 1):
            x_copy(da, db).wait_recv()
            for p, buf in ((same_index(da, db), gs), (other_index(da, db), gb)):
                entries.append(p)
                blocks.append(jnp.where(rsub_ref[0, p] == 0, buf[da, db, 0], buf[da, db, 1]))
        accumulate(entries, blocks)

    def local_tiles(first):
        entries = [REMOTE + first + k for k in range(4)]
        accumulate(entries, [feat[src_ref[0, tab[0, i]]] for i in entries])

    def self_product():
        rows = feat[...].reshape(OWN * BLK, D)
        pre[...] = jnp.dot(rows, ws[...], preferred_element_type=F32) + bias[...]

    z_start()
    a_start()
    b_start(0)
    x_copy(0, 0).start()
    acc[...] = jnp.zeros_like(acc)
    deg[...] = jnp.zeros_like(deg)
    for load in loads:
        load.wait()
    gs[0, 0] = feat[0:2]
    found = find_tiles()
    self_product()
    transpose_tiles(0, 12)
    found.wait()

    z_step(0, True)
    transpose_tiles(12, 12)
    z_step(1, False)
    transpose_tiles(24, 8)
    z_step(1, True)
    a_mid()
    b_mid(0)
    z_pair(1)
    z_step(2, False)
    z_first()
    local_tiles(0)
    z_step(2, True)
    a_end()
    z_pair(2)
    z_step(3, False)
    transpose_tiles(32, 8)
    z_step(3, True)
    b_mid(1)
    b_mid(3)
    b_end(0)
    z_pair(3)
    z_step(4, False)
    transpose_tiles(40, 8)
    sub_pairs(0, 0)
    z_step(4, True)
    b_mid(2)
    b_end(1)
    b_end(3)
    z_pair(4)
    z_step(5, False)
    transpose_tiles(48, 6)
    sub_pairs(0, 2)
    z_step(5, True)
    b_end(2)
    z_pair(5)
    sub_pairs(1, 0)
    z_step(6, False)
    sub_pairs(1, 2)
    transpose_tiles(54, 6)
    local_tiles(4)
    z_step(6, True)
    z_pair(6)
    sub_pairs(3, 0)
    sub_pairs(3, 2)
    z_step(7, False)
    sub_pairs(2, 0)
    sub_pairs(2, 2)
    local_tiles(8)
    invert_degree()
    z_pair(7)
    z_step(7, True)
    z_last()

    mean = (acc[...] * inv[...]).astype(BF)
    v = pre[...] + jnp.dot(mean, wn[...], preferred_element_type=F32)
    k0, k1 = 0.7978845608028654, 0.044715
    square = v * v
    th = jnp.tanh(k0 * v * (1.0 + k1 * square))
    slope = 0.5 * (1.0 + th) + 0.5 * v * (1.0 - th * th) * (k0 * (1.0 + 3.0 * k1 * square))
    grad_pre = (gout[...].astype(F32) * slope).astype(BF)
    spread[...] = (dot_nt(grad_pre, wn[...]) * inv[...]).astype(BF).reshape(OWN, BLK, D)

    def partial(i):
        t = tab[0, i]
        return jnp.dot(wt[t], spread[dst_ref[0, t]], preferred_element_type=F32)

    def only(keep, value):
        return jnp.where(keep, value, jnp.zeros_like(value))

    def k_copy(up_way, d, q):
        out_buf, in_buf, send, recv = (su, ru, ku_s, ku_r) if up_way else (sd, rd, kd_s, kd_r)
        h, rows = rows_of(q)
        slot, device = d - 1, up if up_way else dn
        if SKIP_B and is_far(up_way, q) and d == 2:
            slot, device = 0, up2 if up_way else dn2
        if SKIP_B and is_far(up_way, q) and d == 1:
            slot = 1
        return copy(
            out_buf.at[d - 1, h, rows], in_buf.at[slot, h, rows], send.at[slot, q], recv.at[slot, q], device
        )

    def k_send(up_way, d, q):
        out_buf, in_buf, part = (su, ru, pu) if up_way else (sd, rd, pd)
        h, rows = rows_of(q)
        far = is_far(up_way, q)
        owner = wrap(c + d if up_way else c - d, NZ)
        value = only(rclu_ref[0, owner] == h, part[d - 1, rows])
        if (SKIP_B < d < HALF) if far else d < HALF - 1:
            k_copy(up_way, d + 1, q).wait_recv()
            value = value + in_buf[d, h, rows].astype(F32)
        out_buf[d - 1, h, rows] = value.astype(BF)
        k_copy(up_way, d, q).start()

    def k_step(d, far):
        for q in range(PER):
            for up_way in (True, False):
                k_send(up_way, d, q if far == up_way else q + PER)

    def z_partials(d):
        pu[d - 1] = partial(N_SUB + wrap(c + d, NZ))
        pd[d - 1] = partial(N_SUB + wrap(c - d, NZ))

    def kx_copy(da, db):
        return copy(sb.at[da, db], rb.at[da, db], kx_s.at[da, db], kx_r.at[da, db], sib)

    def x_send(da):
        def body(db, _):
            p = other_index(da, db)
            value = partial(p)
            for h in (0, 1):
                sb[da, db, h] = only(rsub_ref[0, p] == h, value).astype(BF)
            kx_copy(da, db).start()
            return 0

        lax.fori_loop(0, RING, body, 0)

    def kb_copy(da, k):
        source, target, device = (
            (sbp.at[da, 0], rbp.at[da, 0], bm),
            (sbp.at[da, 1], rbp.at[da, 1], bp),
            (sbh.at[da, 0], rbh.at[da, 0], bm),
            (sbh.at[da, 1], rbh.at[da, 1], bp),
        )[k]
        return copy(source, target, kb_s.at[da, k], kb_r.at[da, k], device)

    def ka_copy(k):
        source, target, device = (
            (sap.at[0], rap.at[0], am),
            (sap.at[1], rap.at[1], ap),
            (sah.at[0], rah.at[0], am),
            (sah.at[1], rah.at[1], ap),
        )[k]
        return copy(source, target, ka_s.at[k], ka_r.at[k], device)

    def chip_sum(da, db):
        p = same_index(da, db)
        value = partial(p)
        kx_copy(da, db).wait_recv()
        return [
            only(rsub_ref[0, p] == h, value) + rb[da, db, h].astype(F32) for h in (0, 1)
        ]

    def b_far(da):
        v0, v1 = chip_sum(da, 2)
        sbh[da, 0] = v0.astype(BF)
        kb_copy(da, 2).start()
        sbh[da, 1] = v1.astype(BF)
        kb_copy(da, 3).start()

    def b_near(da):
        v0, v1 = chip_sum(da, 1)
        sbp[da, 0, 1] = v1.astype(BF)
        kb_copy(da, 2).wait_recv()
        sbp[da, 0, 0] = (v0 + rbh[da, 0].astype(F32)).astype(BF)
        kb_copy(da, 0).start()
        v0, v1 = chip_sum(da, 3)
        sbp[da, 1, 0] = v0.astype(BF)
        kb_copy(da, 3).wait_recv()
        sbp[da, 1, 1] = (v1 + rbh[da, 1].astype(F32)).astype(BF)
        kb_copy(da, 1).start()

    def row_sum(da):
        v = chip_sum(da, 0)
        kb_copy(da, 0).wait_recv()
        kb_copy(da, 1).wait_recv()
        return [v[h] + rbp[da, 0, h].astype(F32) + rbp[da, 1, h].astype(F32) for h in (0, 1)]

    def a_far():
        v = row_sum(2)
        sah[0] = v[0].astype(BF)
        ka_copy(2).start()
        sah[1] = v[1].astype(BF)
        ka_copy(3).start()

    def a_near():
        v = row_sum(1)
        ka_copy(2).wait_recv()
        sap[0, 0] = (v[0] + rah[0].astype(F32)).astype(BF)
        sap[0, 1] = v[1].astype(BF)
        ka_copy(0).start()
        v = row_sum(3)
        ka_copy(3).wait_recv()
        sap[1, 0] = v[0].astype(BF)
        sap[1, 1] = (v[1] + rah[1].astype(F32)).astype(BF)
        ka_copy(1).start()

    def add_local():
        def body(k, _):
            i = REMOTE + k
            value = partial(i)
            j = src_ref[0, tab[0, i]]
            for n in range(OWN):
                gself[n] += only(j == n, value)
            return 0

        lax.fori_loop(0, LOCAL, body, 0)
        value = partial(N_SUB + c)
        for h in (0, 1):
            gself[h] += only(rclu_ref[0, c] == h, value)

    z_partials(HALF)
    k_step(HALF, True)
    z_partials(7)
    k_step(7, False)
    z_partials(1)
    if SKIP_B:
        k_step(1, True)
    x_send(2)
    z_partials(6)

    k_step(7, True)
    x_send(1)
    k_step(6, False)
    x_send(3)
    z_partials(5)

    k_step(6, True)
    b_far(2)
    k_step(5, False)
    x_send(0)
    z_partials(4)

    k_step(5, True)
    b_far(1)
    b_far(3)
    k_step(4, False)
    b_far(0)
    z_partials(3)

    k_step(4, True)
    b_near(2)
    k_step(3, False)
    b_near(1)
    z_partials(2)

    k_step(3, True)
    b_near(3)
    k_step(2, False)
    b_near(0)

    k_step(2, True)
    a_far()
    k_step(1, False)
    a_near()
    if not SKIP_B:
        k_step(1, True)
    gself[...] = dot_nt(grad_pre, ws[...]).reshape(OWN, BLK, D)
    add_local()

    v = row_sum(0)
    ka_copy(0).wait_recv()
    ka_copy(1).wait_recv()
    out[2] = gself[2].astype(BF)
    for q in range(CHUNKS):
        h, rows = rows_of(q)
        total = gself[h, rows] + v[h][q % PER * ROWS : (q % PER + 1) * ROWS]
        total = total + rap[0, h, rows].astype(F32) + rap[1, h, rows].astype(F32)
        for up_way, buf in ((True, ru), (False, rd)):
            far = SKIP_B and is_far(up_way, q)
            if far:
                k_copy(up_way, 1, q).wait_recv()
                total = total + buf[1, h, rows].astype(F32)
            k_copy(up_way, 2 if far else 1, q).wait_recv()
            total = total + buf[0, h, rows].astype(F32)
        out[h, rows] = total.astype(BF)

    for d in range(1, HALF + 1):
        for q in range(CHUNKS):
            for up_way in (True, False):
                if has(up_way, d, q):
                    z_copy(up_way, d, q).wait_send()
                    k_copy(up_way, d, q).wait_send()
    for k in range(4):
        a_copy(k).wait_send()
        ka_copy(k).wait_send()
    for da in range(RING):
        for k in range(4):
            b_copy(da, k).wait_send()
            kb_copy(da, k).wait_send()
        for db in range(RING):
            x_copy(da, db).wait_send()
            kx_copy(da, db).wait_send()


def shards(
    features, grad_out, w_self, w_neigh, bias, tile_dst, tile_src, tile_weight, recv_sub, recv_cluster
):
    blk = (BLK, D)
    vmem = pl.BlockSpec(memory_space=pltpu.VMEM)
    sems = [(HALF, CHUNKS)] * 4 + [(4,)] * 2 + [(RING, 4)] * 2 + [(RING, RING)] * 2
    scratch = [
        pltpu.SMEM((1, TILES), jnp.int32),
        pltpu.SMEM((1, TILES), jnp.int32),
        pltpu.SMEM((1, N_SUB), jnp.int32),
        pltpu.SMEM((1, NZ), jnp.int32),
        pltpu.VMEM((OWN,) + blk, BF),
        pltpu.VMEM((OWN * BLK, D), BF),
        pltpu.VMEM((D, D), BF),
        pltpu.VMEM((D, D), BF),
        pltpu.VMEM((1, D), F32),
        pltpu.VMEM((1, TILES), jnp.int32),
        pltpu.VMEM((1, SLOTS), jnp.int32),
        pltpu.VMEM((TILES, BLK, BLK), BF),
        pltpu.VMEM((TILES, BLK, BLK), BF),
        pltpu.SMEM((1, SLOTS), jnp.int32),
        pltpu.VMEM((OWN * BLK, D), F32),
        pltpu.VMEM((OWN * BLK, BLK), F32),
        pltpu.VMEM((OWN * BLK, D), F32),
        pltpu.VMEM((OWN * BLK, D), F32),
        pltpu.VMEM((OWN,) + blk, BF),
        pltpu.VMEM((OWN,) + blk, F32),
        pltpu.VMEM((HALF, 2) + blk, BF),
        pltpu.VMEM((HALF, 2) + blk, BF),
        pltpu.VMEM((RING, RING, 2) + blk, BF),
        pltpu.VMEM((RING, RING, 2) + blk, BF),
        pltpu.VMEM((HALF,) + blk, F32),
        pltpu.VMEM((HALF,) + blk, F32),
        pltpu.VMEM((HALF, 2) + blk, BF),
        pltpu.VMEM((HALF, 2) + blk, BF),
        pltpu.VMEM((HALF, 2) + blk, BF),
        pltpu.VMEM((HALF, 2) + blk, BF),
        pltpu.VMEM((RING, RING, 2) + blk, BF),
        pltpu.VMEM((RING, RING, 2) + blk, BF),
        pltpu.VMEM((RING, 2, 2) + blk, BF),
        pltpu.VMEM((RING, 2) + blk, BF),
        pltpu.VMEM((RING, 2, 2) + blk, BF),
        pltpu.VMEM((RING, 2) + blk, BF),
        pltpu.VMEM((2, 2) + blk, BF),
        pltpu.VMEM((2,) + blk, BF),
        pltpu.VMEM((2, 2) + blk, BF),
        pltpu.VMEM((2,) + blk, BF),
        pltpu.SemaphoreType.DMA((11,)),
    ] + [pltpu.SemaphoreType.DMA(shape) for shape in sems + sems]
    result = pl.pallas_call(
        kernel,
        out_shape=jax.ShapeDtypeStruct((OWN,) + blk, BF),
        in_specs=[pl.BlockSpec(memory_space=pl.ANY)] * 10,
        out_specs=vmem,
        scratch_shapes=scratch,
        compiler_params=pltpu.CompilerParams(
            collective_id=0, has_side_effects=True, vmem_limit_bytes=VMEM_BYTES
        ),
        name="sage_layer",
    )(
        tile_src.reshape(1, TILES), tile_dst.reshape(1, TILES), recv_sub, recv_cluster,
        features.reshape((OWN,) + blk), grad_out, w_self, w_neigh, bias.reshape(1, D), tile_weight,
    )
    return result.reshape(OWN * BLK, D)


def solution(mesh):
    rows = P(("cluster", "sub"), None)
    flat = P(("cluster", "sub"))
    placed = (rows, rows, P(), P(), P(), flat, flat, P(("cluster", "sub"), None, None), rows, rows)
    return jax.shard_map(shards, mesh=mesh, in_specs=placed, out_specs=rows, check_vma=False)
```

```python
import functools

import jax
import jax.numpy as jnp
from jax import lax
from jax.experimental import pallas as pl
from jax.experimental.pallas import tpu as pltpu
from jax.sharding import PartitionSpec as P

MESH = pl.DeviceIdType.MESH
BF = jnp.bfloat16
F32 = jnp.float32
NZ = 16
RING = 4
HALF = NZ // 2
BLK = 128
D = 256
OWN = 3
TILES = 60
N_SUB = 32
REMOTE = N_SUB + NZ
LOCAL = TILES - REMOTE
SLOTS = 128
CHUNKS = 4
PER = CHUNKS // 2
ROWS = BLK // PER
VMEM_BYTES = 62 * 1024 * 1024


def wrap(value, size):
    return lax.rem(value + size, size)


def dot_nt(left, right):
    return lax.dot_general(left, right, (((1,), (1,)), ((), ())), preferred_element_type=F32)


def kernel(
    src_hbm, dst_hbm, rsub_hbm, rclu_hbm,
    feat_hbm, gout_hbm, ws_hbm, wn_hbm, bias_hbm, tiles_hbm,
    out_hbm,
    out, src_ref, dst_ref, rsub_ref, rclu_ref, feat, gout, ws, wn, bias,
    src_row, tab_row, w, wt, tab, acc, deg, pre, inv, spread, gself,
    zu, zd, gs, gb,
    pu, pd, su, sd, ru, rd,
    sb, rb, sbp, sbh, rbp, rbh, sap, sah, rap, rah,
    in_s,
    zu_s, zu_r, zd_s, zd_r, a_s, a_r, b_s, b_r, x_s, x_r,
    ku_s, ku_r, kd_s, kd_r, ka_s, ka_r, kb_s, kb_r, kx_s, kx_r,
):
    c = lax.axis_index("cluster")
    s = lax.axis_index("sub")
    core = lax.rem(s, 2)
    x = lax.rem(s // 2, RING)
    y = s // (2 * RING)
    a = x * (1 - core) + y * core
    b = y * (1 - core) + x * core

    def at(da, db, which):
        aa = wrap(a + da, RING)
        bb = wrap(b + db, RING)
        xx = aa * (1 - core) + bb * core
        yy = bb * (1 - core) + aa * core
        return (yy * RING + xx) * 2 + which

    up = (wrap(c + 1, NZ), s)
    dn = (wrap(c - 1, NZ), s)
    ap = (c, at(1, 0, core))
    am = (c, at(-1, 0, core))
    bp = (c, at(0, 1, core))
    bm = (c, at(0, -1, core))
    sib = (c, at(0, 0, 1 - core))

    def copy(source, target, send, recv, device):
        return pltpu.make_async_remote_copy(
            src_ref=source, dst_ref=target, send_sem=send, recv_sem=recv,
            device_id=device, device_id_type=MESH,
        )

    sent = []

    def start(make, *args):
        make(*args).start()
        sent.append((make, args))

    def drain(keep):
        while len(sent) > keep:
            make, args = sent.pop(0)
            make(*args).wait_send()

    def same_index(da, db):
        return at(-da, -db, core)

    def other_index(da, db):
        return at(-db, -da, 1 - core)

    barrier = pltpu.get_barrier_semaphore()
    for device in (up, dn, ap, am, bp, bm, sib):
        pl.semaphore_signal(barrier, inc=1, device_id=device, device_id_type=MESH)
    inputs = (
        (src_hbm, src_row), (feat_hbm, feat), (ws_hbm, ws), (bias_hbm, bias), (src_hbm, src_ref),
        (dst_hbm, dst_ref), (rsub_hbm, rsub_ref), (rclu_hbm, rclu_ref), (tiles_hbm, w), (wn_hbm, wn),
        (gout_hbm, gout),
    )
    loads = [pltpu.make_async_copy(*pair, in_s.at[k]) for k, pair in enumerate(inputs)]
    for load in loads:
        load.start()
    pl.semaphore_wait(barrier, 7)

    def rows_of(q):
        return q // PER, pl.ds(q % PER * ROWS, ROWS)

    def is_far(up_way, q):
        return (q < PER) == up_way

    def has(up_way, d, q):
        return d < HALF or (d == HALF and is_far(up_way, q))

    def z_copy(up_way, d, q):
        buf, send, recv = (zu, zu_s, zu_r) if up_way else (zd, zd_s, zd_r)
        h, rows = rows_of(q)
        source = buf.at[d - 2, h, rows] if d > 1 else feat_hbm.at[h, rows]
        device = up if up_way else dn
        return copy(source, buf.at[d - 1, h, rows], send.at[d - 1, q], recv.at[d - 1, q], device)

    def z_start():
        for far in (True, False):
            for q in range(PER):
                for up_way in (True, False):
                    start(z_copy, up_way, 1, q if far == up_way else q + PER)

    def z_step(r, far):
        d = r + 1 if far else r
        for q in range(PER):
            for up_way in (True, False):
                p = q if far == up_way else q + PER
                z_copy(up_way, d, p).wait_recv()
                if has(up_way, d + 1, p):
                    start(z_copy, up_way, d + 1, p)

    own = feat_hbm.at[pl.ds(0, 2)]

    def a_copy(k):
        source, target, device = (
            (own, gs.at[1, 0], ap),
            (own, gs.at[3, 0], am),
            (gs.at[1, 0, 0], gs.at[2, 0, 0], ap),
            (gs.at[3, 0, 1], gs.at[2, 0, 1], am),
        )[k]
        return copy(source, target, a_s.at[k], a_r.at[k], device)

    def b_copy(da, k):
        source, target, device = (
            (gs.at[da, 0] if da else own, gs.at[da, 1], bp),
            (gs.at[da, 0] if da else own, gs.at[da, 3], bm),
            (gs.at[da, 1, 0], gs.at[da, 2, 0], bp),
            (gs.at[da, 3, 1], gs.at[da, 2, 1], bm),
        )[k]
        return copy(source, target, b_s.at[da, k], b_r.at[da, k], device)

    def x_copy(da, db):
        source = gs.at[da, db]
        if da == 0 and isinstance(db, int) and db == 0:
            source = own
        return copy(source, gb.at[da, db], x_s.at[da, db], x_r.at[da, db], sib)

    def a_start():
        start(a_copy, 0)
        start(a_copy, 1)

    def a_mid():
        a_copy(0).wait_recv()
        start(a_copy, 2)
        a_copy(1).wait_recv()
        start(a_copy, 3)
        for da in (1, 3):
            b_start(da)
            start(x_copy, da, 0)

    def a_end():
        a_copy(2).wait_recv()
        a_copy(3).wait_recv()
        b_start(2)
        start(x_copy, 2, 0)

    def b_start(da):
        start(b_copy, da, 0)
        start(b_copy, da, 1)

    def b_mid(da):
        b_copy(da, 0).wait_recv()
        start(b_copy, da, 2)
        b_copy(da, 1).wait_recv()
        start(b_copy, da, 3)
        start(x_copy, da, 1)
        start(x_copy, da, 3)

    def b_end(da):
        b_copy(da, 2).wait_recv()
        b_copy(da, 3).wait_recv()
        start(x_copy, da, 2)

    def find_tiles():
        row = lax.broadcasted_iota(jnp.int32, (TILES, TILES), 0)
        col = lax.broadcasted_iota(jnp.int32, (TILES, TILES), 1)
        by_col = jnp.broadcast_to(src_row[...], (TILES, TILES))
        earlier = jnp.where(jnp.logical_and(by_col < OWN, col < row), 1, 0)
        earlier = jnp.sum(earlier, axis=1, keepdims=True)
        src = jnp.broadcast_to(src_row[...], (SLOTS, TILES)).T
        place = jnp.where(src < OWN, REMOTE + earlier, src - OWN)
        tile = lax.broadcasted_iota(jnp.int32, (TILES, SLOTS), 0)
        slot = lax.broadcasted_iota(jnp.int32, (TILES, SLOTS), 1)
        tab_row[...] = jnp.sum(jnp.where(place == slot, tile, 0), axis=0, keepdims=True)
        move = pltpu.make_async_copy(tab_row, tab, in_s.at[len(inputs)])
        move.start()
        return move

    def transpose_tiles(first, count):
        def body(k, _):
            for n in range(4):
                t = first + 4 * k + n
                wt[t] = w[t].T
            return 0

        lax.fori_loop(0, count // 4, body, 0)

    def tile_row(entries):
        tiles = [tab[0, i] for i in entries]
        zero = jnp.zeros((BLK, BLK), BF)
        return jnp.concatenate(
            [
                jnp.concatenate([jnp.where(dst_ref[0, t] == k, w[t], zero) for t in tiles], axis=1)
                for k in range(OWN)
            ],
            axis=0,
        )

    def accumulate(entries, blocks, count=True):
        left = tile_row(entries)
        acc[...] += jnp.dot(left, jnp.concatenate(blocks, axis=0), preferred_element_type=F32)
        if count:
            add_degree(left)

    def add_degree(left):
        ones = jnp.ones((left.shape[1], BLK), BF)
        deg[...] += jnp.dot(left, ones, preferred_element_type=F32)

    def invert_degree():
        late = [wrap(c - 7, NZ), wrap(c + 7, NZ), wrap(c + HALF, NZ), c]
        add_degree(tile_row([N_SUB + r for r in late]))
        scale = 1.0 / (deg[...] + 1.0)
        inv[...] = jnp.concatenate([scale, scale], axis=1)

    def z_pair(d):
        r0, r1 = wrap(c - d, NZ), wrap(c + d, NZ)
        block0 = jnp.where(rclu_ref[0, r0] == 0, zu[d - 1, 0], zu[d - 1, 1])
        block1 = jnp.where(rclu_ref[0, r1] == 0, zd[d - 1, 0], zd[d - 1, 1])
        accumulate([N_SUB + r0, N_SUB + r1], [block0, block1], d < 7)

    def z_last():
        r0 = wrap(c + HALF, NZ)
        block0 = jnp.where(rclu_ref[0, r0] == 0, zu[HALF - 1, 0], zd[HALF - 1, 1])
        block1 = jnp.where(rclu_ref[0, c] == 0, feat[0], feat[1])
        accumulate([N_SUB + r0, N_SUB + c], [block0, block1], False)

    def sub_pairs(da, first):
        entries, blocks = [], []
        for db in (first, first + 1):
            x_copy(da, db).wait_recv()
            for p, buf in ((same_index(da, db), gs), (other_index(da, db), gb)):
                entries.append(p)
                blocks.append(jnp.where(rsub_ref[0, p] == 0, buf[da, db, 0], buf[da, db, 1]))
        accumulate(entries, blocks)

    def local_tiles(first):
        entries = [REMOTE + first + k for k in range(4)]
        accumulate(entries, [feat[src_ref[0, tab[0, i]]] for i in entries])

    def self_product():
        rows = feat[...].reshape(OWN * BLK, D)
        pre[...] = jnp.dot(rows, ws[...], preferred_element_type=F32) + bias[...]

    z_start()
    a_start()
    b_start(0)
    start(x_copy, 0, 0)
    acc[...] = jnp.zeros_like(acc)
    deg[...] = jnp.zeros_like(deg)
    loads[0].wait()
    found = find_tiles()
    for load in loads[1:]:
        load.wait()
    gs[0, 0] = feat[0:2]
    self_product()
    transpose_tiles(0, 12)
    found.wait()

    z_step(0, True)
    transpose_tiles(12, 12)
    z_step(1, False)
    transpose_tiles(24, 8)
    z_step(1, True)
    a_mid()
    b_mid(0)
    z_pair(1)
    z_step(2, False)
    local_tiles(0)
    z_step(2, True)
    a_end()
    z_pair(2)
    z_step(3, False)
    transpose_tiles(32, 8)
    z_step(3, True)
    b_mid(1)
    b_mid(3)
    b_end(0)
    z_pair(3)
    z_step(4, False)
    transpose_tiles(40, 8)
    sub_pairs(0, 0)
    drain(52)
    z_step(4, True)
    b_mid(2)
    b_end(1)
    b_end(3)
    z_pair(4)
    z_step(5, False)
    transpose_tiles(48, 4)
    sub_pairs(0, 2)
    drain(52)
    z_step(5, True)
    b_end(2)
    z_pair(5)
    sub_pairs(1, 0)
    z_step(6, False)
    sub_pairs(1, 2)
    transpose_tiles(52, 8)
    drain(52)
    local_tiles(4)
    z_step(6, True)
    z_pair(6)
    sub_pairs(3, 0)
    sub_pairs(3, 2)
    z_step(7, False)
    sub_pairs(2, 0)
    sub_pairs(2, 2)
    local_tiles(8)
    invert_degree()
    z_pair(7)
    z_step(7, True)
    z_last()

    mean = (acc[...] * inv[...]).astype(BF)
    v = pre[...] + jnp.dot(mean, wn[...], preferred_element_type=F32)
    k0, k1 = 0.7978845608028654, 0.044715
    square = v * v
    th = jnp.tanh(k0 * v * (1.0 + k1 * square))
    slope = 0.5 * (1.0 + th) + 0.5 * v * (1.0 - th * th) * (k0 * (1.0 + 3.0 * k1 * square))
    grad_pre = (gout[...].astype(F32) * slope).astype(BF)
    spread[...] = (dot_nt(grad_pre, wn[...]) * inv[...]).astype(BF).reshape(OWN, BLK, D)

    def partial(i):
        t = tab[0, i]
        return jnp.dot(wt[t], spread[dst_ref[0, t]], preferred_element_type=F32)

    def only(keep, value):
        return jnp.where(keep, value, jnp.zeros_like(value))

    def k_copy(up_way, d, q):
        out_buf, in_buf, send, recv = (su, ru, ku_s, ku_r) if up_way else (sd, rd, kd_s, kd_r)
        h, rows = rows_of(q)
        return copy(
            out_buf.at[d - 1, h, rows], in_buf.at[d - 1, h, rows], send.at[d - 1, q], recv.at[d - 1, q],
            up if up_way else dn,
        )

    def k_send(up_way, d, q):
        out_buf, in_buf, part = (su, ru, pu) if up_way else (sd, rd, pd)
        h, rows = rows_of(q)
        owner = wrap(c + d if up_way else c - d, NZ)
        value = only(rclu_ref[0, owner] == h, part[d - 1, rows])
        if has(up_way, d + 1, q):
            k_copy(up_way, d + 1, q).wait_recv()
            value = value + in_buf[d, h, rows].astype(F32)
        out_buf[d - 1, h, rows] = value.astype(BF)
        start(k_copy, up_way, d, q)

    def k_step(d, far):
        for q in range(PER):
            for up_way in (True, False):
                k_send(up_way, d, q if far == up_way else q + PER)

    def z_partials(d):
        pu[d - 1] = partial(N_SUB + wrap(c + d, NZ))
        pd[d - 1] = pu[d - 1] if d == HALF else partial(N_SUB + wrap(c - d, NZ))

    def kx_copy(da, db):
        return copy(sb.at[da, db], rb.at[da, db], kx_s.at[da, db], kx_r.at[da, db], sib)

    def x_send(da):
        for db in (2, 1, 3, 0):
            p = other_index(da, db)
            value = partial(p)
            for h in (0, 1):
                sb[da, db, h] = only(rsub_ref[0, p] == h, value).astype(BF)
            start(kx_copy, da, db)

    def kb_copy(da, k):
        source, target, device = (
            (sbp.at[da, 0], rbp.at[da, 0], bm),
            (sbp.at[da, 1], rbp.at[da, 1], bp),
            (sbh.at[da, 0], rbh.at[da, 0], bm),
            (sbh.at[da, 1], rbh.at[da, 1], bp),
        )[k]
        return copy(source, target, kb_s.at[da, k], kb_r.at[da, k], device)

    def ka_copy(k):
        source, target, device = (
            (sap.at[0], rap.at[0], am),
            (sap.at[1], rap.at[1], ap),
            (sah.at[0], rah.at[0], am),
            (sah.at[1], rah.at[1], ap),
        )[k]
        return copy(source, target, ka_s.at[k], ka_r.at[k], device)

    def chip_sum(da, db):
        p = same_index(da, db)
        value = partial(p)
        kx_copy(da, db).wait_recv()
        return [
            only(rsub_ref[0, p] == h, value) + rb[da, db, h].astype(F32) for h in (0, 1)
        ]

    def b_far(da):
        v0, v1 = chip_sum(da, 2)
        sbh[da, 0] = v0.astype(BF)
        start(kb_copy, da, 2)
        sbh[da, 1] = v1.astype(BF)
        start(kb_copy, da, 3)

    def b_near(da, db=None):
        if db != 3:
            b_near_1(da)
        if db != 1:
            b_near_3(da)

    def b_near_1(da):
        v0, v1 = chip_sum(da, 1)
        sbp[da, 0, 1] = v1.astype(BF)
        kb_copy(da, 2).wait_recv()
        sbp[da, 0, 0] = (v0 + rbh[da, 0].astype(F32)).astype(BF)
        start(kb_copy, da, 0)

    def b_near_3(da):
        v0, v1 = chip_sum(da, 3)
        sbp[da, 1, 0] = v0.astype(BF)
        kb_copy(da, 3).wait_recv()
        sbp[da, 1, 1] = (v1 + rbh[da, 1].astype(F32)).astype(BF)
        start(kb_copy, da, 1)

    def row_sum(da):
        v = chip_sum(da, 0)
        kb_copy(da, 0).wait_recv()
        kb_copy(da, 1).wait_recv()
        return [v[h] + rbp[da, 0, h].astype(F32) + rbp[da, 1, h].astype(F32) for h in (0, 1)]

    def a_far():
        v = row_sum(2)
        sah[0] = v[0].astype(BF)
        start(ka_copy, 2)
        sah[1] = v[1].astype(BF)
        start(ka_copy, 3)

    def a_near():
        v = row_sum(1)
        ka_copy(2).wait_recv()
        sap[0, 0] = (v[0] + rah[0].astype(F32)).astype(BF)
        sap[0, 1] = v[1].astype(BF)
        start(ka_copy, 0)
        v = row_sum(3)
        ka_copy(3).wait_recv()
        sap[1, 0] = v[0].astype(BF)
        sap[1, 1] = (v[1] + rah[1].astype(F32)).astype(BF)
        start(ka_copy, 1)

    def add_local(first):
        entries = [REMOTE + first + k for k in range(4)]
        values = [partial(i) for i in entries]
        blocks = [src_ref[0, tab[0, i]] for i in entries]
        for n in range(OWN):
            gself[n] += sum(only(j == n, value) for j, value in zip(blocks, values))

    def add_own():
        value = partial(N_SUB + c)
        for h in (0, 1):
            gself[h] += only(rclu_ref[0, c] == h, value)

    def grad_self():
        gself[...] = dot_nt(grad_pre, ws[...]).reshape(OWN, BLK, D)

    z_partials(HALF)
    k_step(HALF, True)
    z_partials(7)
    k_step(7, False)
    x_send(2)
    x_send(1)
    z_partials(6)
    k_step(7, True)
    x_send(3)
    k_step(6, False)
    x_send(0)
    z_partials(5)
    k_step(6, True)
    b_far(2)
    drain(60)
    k_step(5, False)
    b_far(1)
    z_partials(4)
    k_step(5, True)
    b_far(3)
    b_far(0)
    drain(60)
    k_step(4, False)
    b_near(2)
    z_partials(3)
    k_step(4, True)
    b_near(1)
    drain(56)
    k_step(3, False)
    b_near(3)
    z_partials(2)
    k_step(3, True)
    a_far()
    drain(48)
    k_step(2, False)
    b_near(0)
    z_partials(1)
    k_step(2, True)
    grad_self()
    add_local(0)
    drain(40)
    k_step(1, False)
    a_near()
    add_local(4)
    k_step(1, True)
    add_local(8)
    add_own()
    drain(24)

    v = row_sum(0)
    ka_copy(0).wait_recv()
    ka_copy(1).wait_recv()
    puts = []

    def put(h, rows, k):
        puts.append(pltpu.make_async_copy(out.at[h, rows], out_hbm.at[h, rows], in_s.at[k]))
        puts[-1].start()

    out[2] = gself[2].astype(BF)
    put(2, pl.ds(0, BLK), CHUNKS)
    for q in range(CHUNKS):
        h, rows = rows_of(q)
        total = gself[h, rows] + v[h][q % PER * ROWS : (q % PER + 1) * ROWS]
        total = total + rap[0, h, rows].astype(F32) + rap[1, h, rows].astype(F32)
        for up_way, buf in ((True, ru), (False, rd)):
            k_copy(up_way, 1, q).wait_recv()
            total = total + buf[0, h, rows].astype(F32)
        out[h, rows] = total.astype(BF)
        put(h, rows, q)

    drain(0)
    for cp in puts:
        cp.wait()


def shards(
    features, grad_out, w_self, w_neigh, bias, tile_dst, tile_src, tile_weight, recv_sub, recv_cluster
):
    blk = (BLK, D)
    sems = [(HALF, CHUNKS)] * 4 + [(4,)] * 2 + [(RING, 4)] * 2 + [(RING, RING)] * 2
    scratch = [
        pltpu.VMEM((OWN,) + blk, BF),
        pltpu.SMEM((1, TILES), jnp.int32),
        pltpu.SMEM((1, TILES), jnp.int32),
        pltpu.SMEM((1, N_SUB), jnp.int32),
        pltpu.SMEM((1, NZ), jnp.int32),
        pltpu.VMEM((OWN,) + blk, BF),
        pltpu.VMEM((OWN * BLK, D), BF),
        pltpu.VMEM((D, D), BF),
        pltpu.VMEM((D, D), BF),
        pltpu.VMEM((1, D), F32),
        pltpu.VMEM((1, TILES), jnp.int32),
        pltpu.VMEM((1, SLOTS), jnp.int32),
        pltpu.VMEM((TILES, BLK, BLK), BF),
        pltpu.VMEM((TILES, BLK, BLK), BF),
        pltpu.SMEM((1, SLOTS), jnp.int32),
        pltpu.VMEM((OWN * BLK, D), F32),
        pltpu.VMEM((OWN * BLK, BLK), F32),
        pltpu.VMEM((OWN * BLK, D), F32),
        pltpu.VMEM((OWN * BLK, D), F32),
        pltpu.VMEM((OWN,) + blk, BF),
        pltpu.VMEM((OWN,) + blk, F32),
        pltpu.VMEM((HALF, 2) + blk, BF),
        pltpu.VMEM((HALF, 2) + blk, BF),
        pltpu.VMEM((RING, RING, 2) + blk, BF),
        pltpu.VMEM((RING, RING, 2) + blk, BF),
        pltpu.VMEM((HALF,) + blk, F32),
        pltpu.VMEM((HALF,) + blk, F32),
        pltpu.VMEM((HALF, 2) + blk, BF),
        pltpu.VMEM((HALF, 2) + blk, BF),
        pltpu.VMEM((HALF, 2) + blk, BF),
        pltpu.VMEM((HALF, 2) + blk, BF),
        pltpu.VMEM((RING, RING, 2) + blk, BF),
        pltpu.VMEM((RING, RING, 2) + blk, BF),
        pltpu.VMEM((RING, 2, 2) + blk, BF),
        pltpu.VMEM((RING, 2) + blk, BF),
        pltpu.VMEM((RING, 2, 2) + blk, BF),
        pltpu.VMEM((RING, 2) + blk, BF),
        pltpu.VMEM((2, 2) + blk, BF),
        pltpu.VMEM((2,) + blk, BF),
        pltpu.VMEM((2, 2) + blk, BF),
        pltpu.VMEM((2,) + blk, BF),
        pltpu.SemaphoreType.DMA((12,)),
    ] + [pltpu.SemaphoreType.DMA(shape) for shape in sems + sems]
    result = pl.pallas_call(
        kernel,
        out_shape=jax.ShapeDtypeStruct((OWN,) + blk, BF),
        in_specs=[pl.BlockSpec(memory_space=pl.ANY)] * 10,
        out_specs=pl.BlockSpec(memory_space=pl.ANY),
        scratch_shapes=scratch,
        compiler_params=pltpu.CompilerParams(
            collective_id=0, has_side_effects=True, vmem_limit_bytes=VMEM_BYTES
        ),
        name="sage_layer",
    )(
        tile_src.reshape(1, TILES), tile_dst.reshape(1, TILES), recv_sub, recv_cluster,
        features.reshape((OWN,) + blk), grad_out, w_self, w_neigh, bias.reshape(1, D), tile_weight,
    )
    return result.reshape(OWN * BLK, D)


def solution(mesh):
    rows = P(("cluster", "sub"), None)
    flat = P(("cluster", "sub"))
    placed = (rows, rows, P(), P(), P(), flat, flat, P(("cluster", "sub"), None, None), rows, rows)
    return jax.shard_map(shards, mesh=mesh, in_specs=placed, out_specs=rows, check_vma=False)
```

```python
import itertools

import jax
import jax.numpy as jnp
from jax import lax
from jax.experimental import pallas as pl
from jax.experimental.pallas import tpu as pltpu
from jax.sharding import PartitionSpec as P

MESH = pl.DeviceIdType.MESH
BF = jnp.bfloat16
F32 = jnp.float32
NZ = 16
RING = 4
HALF = NZ // 2
BLK = 128
D = 256
OWN = 3
TILES = 60
N_SUB = 32
REMOTE = N_SUB + NZ
LOCAL = TILES - REMOTE
SLOTS = 128
POOL = 40
CHUNKS = 4
PER = CHUNKS // 2
ROWS = BLK // PER
VMEM_BYTES = 62 * 1024 * 1024


def wrap(value, size):
    return lax.rem(value + size, size)


def dot_nt(left, right):
    return lax.dot_general(left, right, (((1,), (1,)), ((), ())), preferred_element_type=F32)


def kernel(
    src_hbm, dst_hbm, rsub_hbm, rclu_hbm,
    feat_hbm, gout_hbm, ws_hbm, wn_hbm, bias_hbm, tiles_hbm,
    out_hbm,
    out, src_ref, dst_ref, rsub_ref, rclu_ref, feat, gout, ws, wn, bias,
    src_row, tab_row, w, wt, tab, acc, deg, pre, inv, spread, gself,
    zu, zd, gs, gb,
    pu, pd, su, sd, ru, rd,
    sb, rb, sbp, sbh, rbp, rbh, sap, sah, rap, rah,
    in_s,
    pool, zu_r, zd_r, a_r, b_r, x_r, ku_r, kd_r, ka_r, kb_r, kx_r,
):
    c = lax.axis_index("cluster")
    s = lax.axis_index("sub")
    core = lax.rem(s, 2)
    x = lax.rem(s // 2, RING)
    y = s // (2 * RING)
    a = x * (1 - core) + y * core
    b = y * (1 - core) + x * core

    def at(da, db, which):
        aa = wrap(a + da, RING)
        bb = wrap(b + db, RING)
        xx = aa * (1 - core) + bb * core
        yy = bb * (1 - core) + aa * core
        return (yy * RING + xx) * 2 + which

    up = (wrap(c + 1, NZ), s)
    dn = (wrap(c - 1, NZ), s)
    ap = (c, at(1, 0, core))
    am = (c, at(-1, 0, core))
    bp = (c, at(0, 1, core))
    bm = (c, at(0, -1, core))
    sib = (c, at(0, 0, 1 - core))

    def copy(source, target, recv, device, lane=0):
        return pltpu.make_async_remote_copy(
            src_ref=source, dst_ref=target, send_sem=pool.at[lane], recv_sem=recv,
            device_id=device, device_id_type=MESH,
        )

    sent = []
    lanes = itertools.cycle(range(POOL))

    def start(make, *args):
        drain(POOL - 1)
        lane = next(lanes)
        make(*args, lane=lane).start()
        sent.append((make, args, lane))

    def drain(keep):
        while len(sent) > keep:
            make, args, lane = sent.pop(0)
            make(*args, lane=lane).wait_send()

    def same_index(da, db):
        return at(-da, -db, core)

    def other_index(da, db):
        return at(-db, -da, 1 - core)

    barrier = pltpu.get_barrier_semaphore()
    for device in (up, dn, ap, am, bp, bm, sib):
        pl.semaphore_signal(barrier, inc=1, device_id=device, device_id_type=MESH)
    inputs = (
        (src_hbm, src_row), (feat_hbm, feat), (ws_hbm, ws), (bias_hbm, bias), (src_hbm, src_ref),
        (dst_hbm, dst_ref), (rsub_hbm, rsub_ref), (rclu_hbm, rclu_ref), (tiles_hbm, w), (wn_hbm, wn),
        (gout_hbm, gout),
    )
    loads = [pltpu.make_async_copy(*pair, in_s.at[k]) for k, pair in enumerate(inputs)]
    for load in loads:
        load.start()
    pl.semaphore_wait(barrier, 7)

    def rows_of(q):
        return q // PER, pl.ds(q % PER * ROWS, ROWS)

    def is_far(up_way, q):
        return (q < PER) == up_way

    def has(up_way, d, q):
        return d < HALF or (d == HALF and is_far(up_way, q))

    def z_copy(up_way, d, q, lane=0):
        buf, recv = (zu, zu_r) if up_way else (zd, zd_r)
        h, rows = rows_of(q)
        source = buf.at[d - 2, h, rows] if d > 1 else feat_hbm.at[h, rows]
        device = up if up_way else dn
        return copy(source, buf.at[d - 1, h, rows], recv.at[d - 1, q], device, lane)

    def z_start():
        for far in (True, False):
            for q in range(PER):
                for up_way in (True, False):
                    start(z_copy, up_way, 1, q if far == up_way else q + PER)

    def z_step(r, far):
        d = r + 1 if far else r
        for q in range(PER):
            for up_way in (True, False):
                p = q if far == up_way else q + PER
                z_copy(up_way, d, p).wait_recv()
                if has(up_way, d + 1, p):
                    start(z_copy, up_way, d + 1, p)

    own = feat_hbm.at[pl.ds(0, 2)]

    def a_copy(k, lane=0):
        source, target, device = (
            (own, gs.at[1, 0], ap),
            (own, gs.at[3, 0], am),
            (gs.at[1, 0, 0], gs.at[2, 0, 0], ap),
            (gs.at[3, 0, 1], gs.at[2, 0, 1], am),
        )[k]
        return copy(source, target, a_r.at[min(k, 2)], device, lane)

    def b_copy(da, k, lane=0):
        source, target, device = (
            (gs.at[da, 0] if da else own, gs.at[da, 1], bp),
            (gs.at[da, 0] if da else own, gs.at[da, 3], bm),
            (gs.at[da, 1, 0], gs.at[da, 2, 0], bp),
            (gs.at[da, 3, 1], gs.at[da, 2, 1], bm),
        )[k]
        return copy(source, target, b_r.at[da, min(k, 2)], device, lane)

    def x_copy(da, db, lane=0):
        source = own if (da, db) == (0, 0) else gs.at[da, db]
        return copy(source, gb.at[da, db], x_r.at[da], sib, lane)

    def a_start():
        start(a_copy, 0)
        start(a_copy, 1)

    def a_mid():
        a_copy(0).wait_recv()
        start(a_copy, 2)
        a_copy(1).wait_recv()
        start(a_copy, 3)
        for da in (1, 3):
            b_start(da)
            start(x_copy, da, 0)

    def a_end():
        copy(gs.at[2, 0], gs.at[2, 0], a_r.at[2], ap).wait_recv()
        b_start(2)
        start(x_copy, 2, 0)

    def b_start(da):
        start(b_copy, da, 0)
        start(b_copy, da, 1)

    def b_mid(da):
        b_copy(da, 0).wait_recv()
        start(b_copy, da, 2)
        b_copy(da, 1).wait_recv()
        start(b_copy, da, 3)
        start(x_copy, da, 1)
        start(x_copy, da, 3)

    def b_end(da):
        copy(gs.at[da, 2], gs.at[da, 2], b_r.at[da, 2], bp).wait_recv()
        start(x_copy, da, 2)

    def find_tiles():
        row = lax.broadcasted_iota(jnp.int32, (TILES, TILES), 0)
        col = lax.broadcasted_iota(jnp.int32, (TILES, TILES), 1)
        by_col = jnp.broadcast_to(src_row[...], (TILES, TILES))
        earlier = jnp.where(jnp.logical_and(by_col < OWN, col < row), 1, 0)
        earlier = jnp.sum(earlier, axis=1, keepdims=True)
        src = jnp.broadcast_to(src_row[...], (SLOTS, TILES)).T
        place = jnp.where(src < OWN, REMOTE + earlier, src - OWN)
        tile = lax.broadcasted_iota(jnp.int32, (TILES, SLOTS), 0)
        slot = lax.broadcasted_iota(jnp.int32, (TILES, SLOTS), 1)
        tab_row[...] = jnp.sum(jnp.where(place == slot, tile, 0), axis=0, keepdims=True)
        move = pltpu.make_async_copy(tab_row, tab, in_s.at[len(inputs)])
        move.start()
        return move

    def transpose_tiles(first, count):
        def body(k, _):
            for n in range(4):
                t = first + 4 * k + n
                wt[t] = w[t].T
            return 0

        lax.fori_loop(0, count // 4, body, 0)

    def tile_row(entries):
        tiles = [tab[0, i] for i in entries]
        zero = jnp.zeros((BLK, BLK), BF)
        return jnp.concatenate(
            [
                jnp.concatenate([jnp.where(dst_ref[0, t] == k, w[t], zero) for t in tiles], axis=1)
                for k in range(OWN)
            ],
            axis=0,
        )

    def accumulate(entries, blocks, count=True):
        left = tile_row(entries)
        acc[...] += jnp.dot(left, jnp.concatenate(blocks, axis=0), preferred_element_type=F32)
        if count:
            add_degree(left)

    def add_degree(left):
        ones = jnp.ones((left.shape[1], BLK), BF)
        deg[...] += jnp.dot(left, ones, preferred_element_type=F32)

    def invert_degree():
        late = [wrap(c - 7, NZ), wrap(c + 7, NZ), wrap(c + HALF, NZ), c]
        add_degree(tile_row([N_SUB + r for r in late]))
        scale = 1.0 / (deg[...] + 1.0)
        inv[...] = jnp.concatenate([scale, scale], axis=1)

    def z_pair(d):
        r0, r1 = wrap(c - d, NZ), wrap(c + d, NZ)
        block0 = jnp.where(rclu_ref[0, r0] == 0, zu[d - 1, 0], zu[d - 1, 1])
        block1 = jnp.where(rclu_ref[0, r1] == 0, zd[d - 1, 0], zd[d - 1, 1])
        accumulate([N_SUB + r0, N_SUB + r1], [block0, block1], d < 7)

    def z_last():
        r0 = wrap(c + HALF, NZ)
        block0 = jnp.where(rclu_ref[0, r0] == 0, zu[HALF - 1, 0], zd[HALF - 1, 1])
        block1 = jnp.where(rclu_ref[0, c] == 0, feat[0], feat[1])
        accumulate([N_SUB + r0, N_SUB + c], [block0, block1], False)

    def sub_pairs(da, first):
        entries, blocks = [], []
        if first == 0:
            copy(gb.at[da], gb.at[da], x_r.at[da], sib).wait_recv()
        for db in (first, first + 1):
            for p, buf in ((same_index(da, db), gs), (other_index(da, db), gb)):
                entries.append(p)
                blocks.append(jnp.where(rsub_ref[0, p] == 0, buf[da, db, 0], buf[da, db, 1]))
        accumulate(entries, blocks)

    def local_tiles(first):
        entries = [REMOTE + first + k for k in range(4)]
        accumulate(entries, [feat[src_ref[0, tab[0, i]]] for i in entries])

    def self_product():
        rows = feat[...].reshape(OWN * BLK, D)
        pre[...] = jnp.dot(rows, ws[...], preferred_element_type=F32) + bias[...]

    z_start()
    a_start()
    b_start(0)
    start(x_copy, 0, 0)
    acc[...] = jnp.zeros_like(acc)
    deg[...] = jnp.zeros_like(deg)
    loads[0].wait()
    found = find_tiles()
    for load in loads[1:]:
        load.wait()
    gs[0, 0] = feat[0:2]
    self_product()
    transpose_tiles(0, 12)
    found.wait()

    z_step(0, True)
    transpose_tiles(12, 12)
    z_step(1, False)
    transpose_tiles(24, 8)
    z_step(1, True)
    a_mid()
    b_mid(0)
    z_pair(1)
    z_step(2, False)
    local_tiles(0)
    z_step(2, True)
    a_end()
    z_pair(2)
    z_step(3, False)
    transpose_tiles(32, 8)
    z_step(3, True)
    b_mid(1)
    b_mid(3)
    b_end(0)
    z_pair(3)
    z_step(4, False)
    transpose_tiles(40, 8)
    sub_pairs(0, 0)
    drain(32)
    z_step(4, True)
    b_mid(2)
    b_end(1)
    b_end(3)
    z_pair(4)
    z_step(5, False)
    transpose_tiles(48, 4)
    sub_pairs(0, 2)
    drain(32)
    z_step(5, True)
    b_end(2)
    z_pair(5)
    sub_pairs(1, 0)
    z_step(6, False)
    sub_pairs(1, 2)
    transpose_tiles(52, 8)
    drain(32)
    local_tiles(4)
    z_step(6, True)
    z_pair(6)
    sub_pairs(3, 0)
    sub_pairs(3, 2)
    z_step(7, False)
    sub_pairs(2, 0)
    sub_pairs(2, 2)
    local_tiles(8)
    invert_degree()
    z_pair(7)
    z_step(7, True)
    z_last()

    mean = (acc[...] * inv[...]).astype(BF)
    v = pre[...] + jnp.dot(mean, wn[...], preferred_element_type=F32)
    k0, k1 = 0.7978845608028654, 0.044715
    square = v * v
    th = jnp.tanh(k0 * v * (1.0 + k1 * square))
    slope = 0.5 * (1.0 + th) + 0.5 * v * (1.0 - th * th) * (k0 * (1.0 + 3.0 * k1 * square))
    grad_pre = (gout[...].astype(F32) * slope).astype(BF)
    spread[...] = (dot_nt(grad_pre, wn[...]) * inv[...]).astype(BF).reshape(OWN, BLK, D)

    def partial(i):
        t = tab[0, i]
        return jnp.dot(wt[t], spread[dst_ref[0, t]], preferred_element_type=F32)

    def only(keep, value):
        return jnp.where(keep, value, jnp.zeros_like(value))

    def k_copy(up_way, d, q, lane=0):
        out_buf, in_buf, recv = (su, ru, ku_r) if up_way else (sd, rd, kd_r)
        h, rows = rows_of(q)
        return copy(
            out_buf.at[d - 1, h, rows], in_buf.at[d - 1, h, rows], recv.at[d - 1, q],
            up if up_way else dn, lane,
        )

    def k_send(up_way, d, q):
        out_buf, in_buf, part = (su, ru, pu) if up_way else (sd, rd, pd)
        h, rows = rows_of(q)
        owner = wrap(c + d if up_way else c - d, NZ)
        value = only(rclu_ref[0, owner] == h, part[d - 1, rows])
        if has(up_way, d + 1, q):
            k_copy(up_way, d + 1, q).wait_recv()
            value = value + in_buf[d, h, rows].astype(F32)
        out_buf[d - 1, h, rows] = value.astype(BF)
        start(k_copy, up_way, d, q)

    def k_step(d, far):
        for q in range(PER):
            for up_way in (True, False):
                k_send(up_way, d, q if far == up_way else q + PER)

    def z_partials(d):
        pu[d - 1] = partial(N_SUB + wrap(c + d, NZ))
        pd[d - 1] = pu[d - 1] if d == HALF else partial(N_SUB + wrap(c - d, NZ))

    def kx_copy(da, db, lane=0):
        return copy(sb.at[da, db], rb.at[da, db], kx_r.at[da], sib, lane)

    def x_send(da):
        for db in (2, 1, 3, 0):
            p = other_index(da, db)
            value = partial(p)
            for h in (0, 1):
                sb[da, db, h] = only(rsub_ref[0, p] == h, value).astype(BF)
            start(kx_copy, da, db)

    def kb_copy(da, k, lane=0):
        source, target, device = (
            (sbp.at[da, 0], rbp.at[da, 0], bm),
            (sbp.at[da, 1], rbp.at[da, 1], bp),
            (sbh.at[da, 0], rbh.at[da, 0], bm),
            (sbh.at[da, 1], rbh.at[da, 1], bp),
        )[k]
        return copy(source, target, kb_r.at[da, k], device, lane)

    def ka_copy(k, lane=0):
        source, target, device = (
            (sap.at[0], rap.at[0], am),
            (sap.at[1], rap.at[1], ap),
            (sah.at[0], rah.at[0], am),
            (sah.at[1], rah.at[1], ap),
        )[k]
        return copy(source, target, ka_r.at[k], device, lane)

    def chip_sum(da, db):
        p = same_index(da, db)
        value = partial(p)
        if db == 2:
            copy(rb.at[da], rb.at[da], kx_r.at[da], sib).wait_recv()
        return [
            only(rsub_ref[0, p] == h, value) + rb[da, db, h].astype(F32) for h in (0, 1)
        ]

    def b_far(da):
        v0, v1 = chip_sum(da, 2)
        sbh[da, 0] = v0.astype(BF)
        start(kb_copy, da, 2)
        sbh[da, 1] = v1.astype(BF)
        start(kb_copy, da, 3)

    def b_near(da, db=None):
        if db != 3:
            b_near_1(da)
        if db != 1:
            b_near_3(da)

    def b_near_1(da):
        v0, v1 = chip_sum(da, 1)
        sbp[da, 0, 1] = v1.astype(BF)
        kb_copy(da, 2).wait_recv()
        sbp[da, 0, 0] = (v0 + rbh[da, 0].astype(F32)).astype(BF)
        start(kb_copy, da, 0)

    def b_near_3(da):
        v0, v1 = chip_sum(da, 3)
        sbp[da, 1, 0] = v0.astype(BF)
        kb_copy(da, 3).wait_recv()
        sbp[da, 1, 1] = (v1 + rbh[da, 1].astype(F32)).astype(BF)
        start(kb_copy, da, 1)

    def row_sum(da):
        v = chip_sum(da, 0)
        kb_copy(da, 0).wait_recv()
        kb_copy(da, 1).wait_recv()
        return [v[h] + rbp[da, 0, h].astype(F32) + rbp[da, 1, h].astype(F32) for h in (0, 1)]

    def a_far():
        v = row_sum(2)
        sah[0] = v[0].astype(BF)
        start(ka_copy, 2)
        sah[1] = v[1].astype(BF)
        start(ka_copy, 3)

    def a_near():
        v = row_sum(1)
        ka_copy(2).wait_recv()
        sap[0, 0] = (v[0] + rah[0].astype(F32)).astype(BF)
        sap[0, 1] = v[1].astype(BF)
        start(ka_copy, 0)
        v = row_sum(3)
        ka_copy(3).wait_recv()
        sap[1, 0] = v[0].astype(BF)
        sap[1, 1] = (v[1] + rah[1].astype(F32)).astype(BF)
        start(ka_copy, 1)

    def add_local(first):
        entries = [REMOTE + first + k for k in range(4)]
        values = [partial(i) for i in entries]
        blocks = [src_ref[0, tab[0, i]] for i in entries]
        for n in range(OWN):
            gself[n] += sum(only(j == n, value) for j, value in zip(blocks, values))

    def add_own():
        value = partial(N_SUB + c)
        for h in (0, 1):
            gself[h] += only(rclu_ref[0, c] == h, value)

    def grad_self():
        gself[...] = dot_nt(grad_pre, ws[...]).reshape(OWN, BLK, D)

    z_partials(HALF)
    k_step(HALF, True)
    z_partials(7)
    k_step(7, False)
    x_send(2)
    x_send(1)
    z_partials(6)
    k_step(7, True)
    x_send(3)
    k_step(6, False)
    x_send(0)
    z_partials(5)
    k_step(6, True)
    b_far(2)
    drain(32)
    k_step(5, False)
    b_far(1)
    z_partials(4)
    k_step(5, True)
    b_far(3)
    b_far(0)
    drain(32)
    k_step(4, False)
    b_near(2)
    z_partials(3)
    k_step(4, True)
    b_near(1)
    drain(32)
    k_step(3, False)
    b_near(3)
    z_partials(2)
    k_step(3, True)
    a_far()
    drain(32)
    k_step(2, False)
    b_near(0)
    z_partials(1)
    k_step(2, True)
    grad_self()
    add_local(0)
    drain(28)
    k_step(1, False)
    a_near()
    add_local(4)
    k_step(1, True)
    add_local(8)
    add_own()
    drain(16)

    v = row_sum(0)
    ka_copy(0).wait_recv()
    ka_copy(1).wait_recv()
    puts = []

    def put(h, rows, k):
        puts.append(pltpu.make_async_copy(out.at[h, rows], out_hbm.at[h, rows], in_s.at[k]))
        puts[-1].start()

    out[2] = gself[2].astype(BF)
    put(2, pl.ds(0, BLK), CHUNKS)
    for q in range(CHUNKS):
        h, rows = rows_of(q)
        total = gself[h, rows] + v[h][q % PER * ROWS : (q % PER + 1) * ROWS]
        total = total + rap[0, h, rows].astype(F32) + rap[1, h, rows].astype(F32)
        for up_way, buf in ((True, ru), (False, rd)):
            k_copy(up_way, 1, q).wait_recv()
            total = total + buf[0, h, rows].astype(F32)
        out[h, rows] = total.astype(BF)
        put(h, rows, q)

    drain(0)
    for cp in puts:
        cp.wait()


def shards(
    features, grad_out, w_self, w_neigh, bias, tile_dst, tile_src, tile_weight, recv_sub, recv_cluster
):
    blk = (BLK, D)
    ring_sems = [(HALF, CHUNKS)] * 2
    sems = [(POOL,)] + ring_sems + [(3,), (RING, 3), (RING,)] + ring_sems + [(4,), (RING, 4), (RING,)]
    scratch = [
        pltpu.VMEM((OWN,) + blk, BF),
        pltpu.SMEM((1, TILES), jnp.int32),
        pltpu.SMEM((1, TILES), jnp.int32),
        pltpu.SMEM((1, N_SUB), jnp.int32),
        pltpu.SMEM((1, NZ), jnp.int32),
        pltpu.VMEM((OWN,) + blk, BF),
        pltpu.VMEM((OWN * BLK, D), BF),
        pltpu.VMEM((D, D), BF),
        pltpu.VMEM((D, D), BF),
        pltpu.VMEM((1, D), F32),
        pltpu.VMEM((1, TILES), jnp.int32),
        pltpu.VMEM((1, SLOTS), jnp.int32),
        pltpu.VMEM((TILES, BLK, BLK), BF),
        pltpu.VMEM((TILES, BLK, BLK), BF),
        pltpu.SMEM((1, SLOTS), jnp.int32),
        pltpu.VMEM((OWN * BLK, D), F32),
        pltpu.VMEM((OWN * BLK, BLK), F32),
        pltpu.VMEM((OWN * BLK, D), F32),
        pltpu.VMEM((OWN * BLK, D), F32),
        pltpu.VMEM((OWN,) + blk, BF),
        pltpu.VMEM((OWN,) + blk, F32),
        pltpu.VMEM((HALF, 2) + blk, BF),
        pltpu.VMEM((HALF, 2) + blk, BF),
        pltpu.VMEM((RING, RING, 2) + blk, BF),
        pltpu.VMEM((RING, RING, 2) + blk, BF),
        pltpu.VMEM((HALF,) + blk, F32),
        pltpu.VMEM((HALF,) + blk, F32),
        pltpu.VMEM((HALF, 2) + blk, BF),
        pltpu.VMEM((HALF, 2) + blk, BF),
        pltpu.VMEM((HALF, 2) + blk, BF),
        pltpu.VMEM((HALF, 2) + blk, BF),
        pltpu.VMEM((RING, RING, 2) + blk, BF),
        pltpu.VMEM((RING, RING, 2) + blk, BF),
        pltpu.VMEM((RING, 2, 2) + blk, BF),
        pltpu.VMEM((RING, 2) + blk, BF),
        pltpu.VMEM((RING, 2, 2) + blk, BF),
        pltpu.VMEM((RING, 2) + blk, BF),
        pltpu.VMEM((2, 2) + blk, BF),
        pltpu.VMEM((2,) + blk, BF),
        pltpu.VMEM((2, 2) + blk, BF),
        pltpu.VMEM((2,) + blk, BF),
        pltpu.SemaphoreType.DMA((12,)),
    ] + [pltpu.SemaphoreType.DMA(shape) for shape in sems]
    result = pl.pallas_call(
        kernel,
        out_shape=jax.ShapeDtypeStruct((OWN,) + blk, BF),
        in_specs=[pl.BlockSpec(memory_space=pl.ANY)] * 10,
        out_specs=pl.BlockSpec(memory_space=pl.ANY),
        scratch_shapes=scratch,
        compiler_params=pltpu.CompilerParams(
            collective_id=0, has_side_effects=True, vmem_limit_bytes=VMEM_BYTES
        ),
        name="sage_layer",
    )(
        tile_src.reshape(1, TILES), tile_dst.reshape(1, TILES), recv_sub, recv_cluster,
        features.reshape((OWN,) + blk), grad_out, w_self, w_neigh, bias.reshape(1, D), tile_weight,
    )
    return result.reshape(OWN * BLK, D)


def solution(mesh):
    rows = P(("cluster", "sub"), None)
    flat = P(("cluster", "sub"))
    placed = (rows, rows, P(), P(), P(), flat, flat, P(("cluster", "sub"), None, None), rows, rows)
    return jax.shard_map(shards, mesh=mesh, in_specs=placed, out_specs=rows, check_vma=False)
```

```python
import itertools

import jax
import jax.numpy as jnp
from jax import lax
from jax.experimental import pallas as pl
from jax.experimental.pallas import tpu as pltpu
from jax.sharding import PartitionSpec as P

MESH = pl.DeviceIdType.MESH
BF = jnp.bfloat16
F32 = jnp.float32
NZ = 16
RING = 4
HALF = NZ // 2
BLK = 128
D = 256
OWN = 3
TILES = 60
N_SUB = 32
REMOTE = N_SUB + NZ
LOCAL = TILES - REMOTE
SLOTS = 128
POOL = 40
CHUNKS = 4
PER = CHUNKS // 2
ROWS = BLK // PER
VMEM_BYTES = 62 * 1024 * 1024


def wrap(value, size):
    return lax.rem(value + size, size)


def dot_nt(left, right):
    return lax.dot_general(left, right, (((1,), (1,)), ((), ())), preferred_element_type=F32)


def kernel(
    src_hbm, dst_hbm, rsub_hbm, rclu_hbm,
    feat_hbm, gout_hbm, ws_hbm, wn_hbm, bias_hbm, tiles_hbm,
    out_hbm,
    out, src_ref, dst_ref, rsub_ref, rclu_ref, feat, gout, ws, wn, bias,
    src_row, tab_row, w, wt, tab, acc, deg, pre, inv, spread, gself,
    zu, zd, gs, gb,
    pu, pd, su, sd, ru, rd,
    sb, rb, sbp, sbh, rbp, rbh, sap, sah, rap, rah,
    in_s,
    pool, zu_r, zd_r, a_r, b_r, x_r, k_r, ka_r, kb_r, kx_r,
):
    c = lax.axis_index("cluster")
    s = lax.axis_index("sub")
    core = lax.rem(s, 2)
    x = lax.rem(s // 2, RING)
    y = s // (2 * RING)
    a = x * (1 - core) + y * core
    b = y * (1 - core) + x * core

    def at(da, db, which):
        aa = wrap(a + da, RING)
        bb = wrap(b + db, RING)
        xx = aa * (1 - core) + bb * core
        yy = bb * (1 - core) + aa * core
        return (yy * RING + xx) * 2 + which

    up = (wrap(c + 1, NZ), s)
    dn = (wrap(c - 1, NZ), s)
    ap = (c, at(1, 0, core))
    am = (c, at(-1, 0, core))
    bp = (c, at(0, 1, core))
    bm = (c, at(0, -1, core))
    sib = (c, at(0, 0, 1 - core))

    def copy(source, target, recv, device, lane=0):
        return pltpu.make_async_remote_copy(
            src_ref=source, dst_ref=target, send_sem=pool.at[lane], recv_sem=recv,
            device_id=device, device_id_type=MESH,
        )

    sent = []
    lanes = itertools.cycle(range(POOL))

    def start(make, *args):
        drain(POOL - 1)
        lane = next(lanes)
        make(*args, lane=lane).start()
        sent.append((make, args, lane))

    def drain(keep):
        while len(sent) > keep:
            make, args, lane = sent.pop(0)
            make(*args, lane=lane).wait_send()

    def same_index(da, db):
        return at(-da, -db, core)

    def other_index(da, db):
        return at(-db, -da, 1 - core)

    barrier = pltpu.get_barrier_semaphore()
    for device in (up, dn, ap, am, bp, bm, sib):
        pl.semaphore_signal(barrier, inc=1, device_id=device, device_id_type=MESH)
    inputs = (
        (src_hbm, src_row), (feat_hbm, feat), (ws_hbm, ws), (bias_hbm, bias), (src_hbm, src_ref),
        (dst_hbm, dst_ref), (rsub_hbm, rsub_ref), (rclu_hbm, rclu_ref), (tiles_hbm, w), (wn_hbm, wn),
        (gout_hbm, gout),
    )
    loads = [pltpu.make_async_copy(*pair, in_s.at[k]) for k, pair in enumerate(inputs)]
    for load in loads:
        load.start()
    pl.semaphore_wait(barrier, 7)

    def rows_of(q):
        return q // PER, pl.ds(q % PER * ROWS, ROWS)

    def is_far(up_way, q):
        return (q < PER) == up_way

    def has(up_way, d, q):
        return d < HALF or (d == HALF and is_far(up_way, q))

    def z_copy(up_way, d, q, lane=0):
        buf, recv = (zu, zu_r) if up_way else (zd, zd_r)
        h, rows = rows_of(q)
        source = buf.at[d - 2, h, rows] if d > 1 else feat_hbm.at[h, rows]
        device = up if up_way else dn
        return copy(source, buf.at[d - 1, h, rows], recv.at[d - 1, q], device, lane)

    def z_start():
        for far in (True, False):
            for q in range(PER):
                for up_way in (True, False):
                    start(z_copy, up_way, 1, q if far == up_way else q + PER)

    def z_step(r, far):
        d = r + 1 if far else r
        for q in range(PER):
            for up_way in (True, False):
                p = q if far == up_way else q + PER
                z_copy(up_way, d, p).wait_recv()
                if has(up_way, d + 1, p):
                    start(z_copy, up_way, d + 1, p)

    own = feat_hbm.at[pl.ds(0, 2)]

    def a_copy(k, lane=0):
        source, target, device = (
            (own, gs.at[1, 0], ap),
            (own, gs.at[3, 0], am),
            (gs.at[1, 0, 0], gs.at[2, 0, 0], ap),
            (gs.at[3, 0, 1], gs.at[2, 0, 1], am),
        )[k]
        return copy(source, target, a_r.at[min(k, 2)], device, lane)

    def b_copy(da, k, lane=0):
        source, target, device = (
            (gs.at[da, 0] if da else own, gs.at[da, 1], bp),
            (gs.at[da, 0] if da else own, gs.at[da, 3], bm),
            (gs.at[da, 1, 0], gs.at[da, 2, 0], bp),
            (gs.at[da, 3, 1], gs.at[da, 2, 1], bm),
        )[k]
        return copy(source, target, b_r.at[da, min(k, 2)], device, lane)

    def x_copy(da, db, lane=0):
        source = own if (da, db) == (0, 0) else gs.at[da, db]
        return copy(source, gb.at[da, db], x_r.at[da], sib, lane)

    def a_start():
        start(a_copy, 0)
        start(a_copy, 1)

    def a_mid():
        a_copy(0).wait_recv()
        start(a_copy, 2)
        a_copy(1).wait_recv()
        start(a_copy, 3)
        for da in (1, 3):
            b_start(da)
            start(x_copy, da, 0)

    def a_end():
        copy(gs.at[2, 0], gs.at[2, 0], a_r.at[2], ap).wait_recv()
        b_start(2)
        start(x_copy, 2, 0)

    def b_start(da):
        start(b_copy, da, 0)
        start(b_copy, da, 1)

    def b_mid(da):
        b_copy(da, 0).wait_recv()
        start(b_copy, da, 2)
        b_copy(da, 1).wait_recv()
        start(b_copy, da, 3)
        start(x_copy, da, 1)
        start(x_copy, da, 3)

    def b_end(da):
        copy(gs.at[da, 2], gs.at[da, 2], b_r.at[da, 2], bp).wait_recv()
        start(x_copy, da, 2)

    def find_tiles():
        row = lax.broadcasted_iota(jnp.int32, (TILES, TILES), 0)
        col = lax.broadcasted_iota(jnp.int32, (TILES, TILES), 1)
        by_col = jnp.broadcast_to(src_row[...], (TILES, TILES))
        earlier = jnp.where(jnp.logical_and(by_col < OWN, col < row), 1, 0)
        earlier = jnp.sum(earlier, axis=1, keepdims=True)
        src = jnp.broadcast_to(src_row[...], (SLOTS, TILES)).T
        place = jnp.where(src < OWN, REMOTE + earlier, src - OWN)
        tile = lax.broadcasted_iota(jnp.int32, (TILES, SLOTS), 0)
        slot = lax.broadcasted_iota(jnp.int32, (TILES, SLOTS), 1)
        tab_row[...] = jnp.sum(jnp.where(place == slot, tile, 0), axis=0, keepdims=True)
        move = pltpu.make_async_copy(tab_row, tab, in_s.at[len(inputs)])
        move.start()
        return move

    def transpose_tiles(first, count):
        def body(k, _):
            for n in range(4):
                t = first + 4 * k + n
                wt[t] = w[t].T
            return 0

        lax.fori_loop(0, count // 4, body, 0)

    def tile_row(entries):
        tiles = [tab[0, i] for i in entries]
        zero = jnp.zeros((BLK, BLK), BF)
        return jnp.concatenate(
            [
                jnp.concatenate([jnp.where(dst_ref[0, t] == k, w[t], zero) for t in tiles], axis=1)
                for k in range(OWN)
            ],
            axis=0,
        )

    def accumulate(entries, blocks, count=True):
        left = tile_row(entries)
        acc[...] += jnp.dot(left, jnp.concatenate(blocks, axis=0), preferred_element_type=F32)
        if count:
            add_degree(left)

    def add_degree(left):
        ones = jnp.ones((left.shape[1], BLK), BF)
        deg[...] += jnp.dot(left, ones, preferred_element_type=F32)

    def invert_degree():
        late = [wrap(c - 7, NZ), wrap(c + 7, NZ), wrap(c + HALF, NZ), c]
        add_degree(tile_row([N_SUB + r for r in late]))
        scale = 1.0 / (deg[...] + 1.0)
        inv[...] = jnp.concatenate([scale, scale], axis=1)

    def z_pair(d):
        r0, r1 = wrap(c - d, NZ), wrap(c + d, NZ)
        block0 = jnp.where(rclu_ref[0, r0] == 0, zu[d - 1, 0], zu[d - 1, 1])
        block1 = jnp.where(rclu_ref[0, r1] == 0, zd[d - 1, 0], zd[d - 1, 1])
        accumulate([N_SUB + r0, N_SUB + r1], [block0, block1], d < 7)

    def z_last():
        r0 = wrap(c + HALF, NZ)
        block0 = jnp.where(rclu_ref[0, r0] == 0, zu[HALF - 1, 0], zd[HALF - 1, 1])
        block1 = jnp.where(rclu_ref[0, c] == 0, feat[0], feat[1])
        accumulate([N_SUB + r0, N_SUB + c], [block0, block1], False)

    def sub_pairs(da, first):
        entries, blocks = [], []
        if first == 0:
            copy(gb.at[da], gb.at[da], x_r.at[da], sib).wait_recv()
        for db in (first, first + 1):
            for p, buf in ((same_index(da, db), gs), (other_index(da, db), gb)):
                entries.append(p)
                blocks.append(jnp.where(rsub_ref[0, p] == 0, buf[da, db, 0], buf[da, db, 1]))
        accumulate(entries, blocks)

    def local_tiles(first):
        entries = [REMOTE + first + k for k in range(4)]
        accumulate(entries, [feat[src_ref[0, tab[0, i]]] for i in entries])

    def self_product():
        rows = feat[...].reshape(OWN * BLK, D)
        pre[...] = jnp.dot(rows, ws[...], preferred_element_type=F32) + bias[...]

    z_start()
    a_start()
    b_start(0)
    start(x_copy, 0, 0)
    acc[...] = jnp.zeros_like(acc)
    deg[...] = jnp.zeros_like(deg)
    loads[0].wait()
    found = find_tiles()
    for load in loads[1:]:
        load.wait()
    gs[0, 0] = feat[0:2]
    self_product()
    transpose_tiles(0, 12)
    found.wait()

    z_step(0, True)
    transpose_tiles(12, 12)
    z_step(1, False)
    transpose_tiles(24, 8)
    z_step(1, True)
    a_mid()
    b_mid(0)
    z_pair(1)
    z_step(2, False)
    local_tiles(0)
    z_step(2, True)
    a_end()
    z_pair(2)
    z_step(3, False)
    transpose_tiles(32, 8)
    z_step(3, True)
    b_mid(1)
    b_mid(3)
    b_end(0)
    z_pair(3)
    z_step(4, False)
    transpose_tiles(40, 8)
    sub_pairs(0, 0)
    drain(32)
    z_step(4, True)
    b_mid(2)
    b_end(1)
    b_end(3)
    z_pair(4)
    z_step(5, False)
    transpose_tiles(48, 4)
    sub_pairs(0, 2)
    drain(32)
    z_step(5, True)
    b_end(2)
    z_pair(5)
    sub_pairs(1, 0)
    z_step(6, False)
    sub_pairs(1, 2)
    transpose_tiles(52, 8)
    drain(32)
    local_tiles(4)
    z_step(6, True)
    z_pair(6)
    sub_pairs(3, 0)
    sub_pairs(3, 2)
    z_step(7, False)
    sub_pairs(2, 0)
    sub_pairs(2, 2)
    local_tiles(8)
    invert_degree()
    z_pair(7)
    z_step(7, True)
    z_last()

    mean = (acc[...] * inv[...]).astype(BF)
    v = pre[...] + jnp.dot(mean, wn[...], preferred_element_type=F32)
    k0, k1 = 0.7978845608028654, 0.044715
    square = v * v
    th = jnp.tanh(k0 * v * (1.0 + k1 * square))
    slope = 0.5 * (1.0 + th) + 0.5 * v * (1.0 - th * th) * (k0 * (1.0 + 3.0 * k1 * square))
    grad_pre = (gout[...].astype(F32) * slope).astype(BF)
    spread[...] = (dot_nt(grad_pre, wn[...]) * inv[...]).astype(BF).reshape(OWN, BLK, D)

    def partial(i):
        t = tab[0, i]
        return jnp.dot(wt[t], spread[dst_ref[0, t]], preferred_element_type=F32)

    def only(keep, value):
        return jnp.where(keep, value, jnp.zeros_like(value))

    def k_recv(up_way, d, q):
        if d == 7 and is_far(up_way, q):
            return k_r.at[q]
        return (zd_r if up_way else zu_r).at[d - 1, q]

    def k_copy(up_way, d, q, lane=0):
        out_buf, in_buf = (su, ru) if up_way else (sd, rd)
        h, rows = rows_of(q)
        return copy(
            out_buf.at[d - 1, h, rows], in_buf.at[d - 1, h, rows], k_recv(up_way, d, q),
            up if up_way else dn, lane,
        )

    def k_send(up_way, d, q):
        out_buf, in_buf, part = (su, ru, pu) if up_way else (sd, rd, pd)
        h, rows = rows_of(q)
        owner = wrap(c + d if up_way else c - d, NZ)
        value = only(rclu_ref[0, owner] == h, part[d - 1, rows])
        if has(up_way, d + 1, q):
            k_copy(up_way, d + 1, q).wait_recv()
            value = value + in_buf[d, h, rows].astype(F32)
        out_buf[d - 1, h, rows] = value.astype(BF)
        start(k_copy, up_way, d, q)

    def k_step(d, far):
        for q in range(PER):
            for up_way in (True, False):
                k_send(up_way, d, q if far == up_way else q + PER)

    def z_partials(d):
        pu[d - 1] = partial(N_SUB + wrap(c + d, NZ))
        pd[d - 1] = pu[d - 1] if d == HALF else partial(N_SUB + wrap(c - d, NZ))

    def kx_copy(da, db, lane=0):
        return copy(sb.at[da, db], rb.at[da, db], kx_r.at[da], sib, lane)

    def x_send(da):
        for db in (2, 1, 3, 0):
            p = other_index(da, db)
            value = partial(p)
            for h in (0, 1):
                sb[da, db, h] = only(rsub_ref[0, p] == h, value).astype(BF)
            start(kx_copy, da, db)

    def kb_copy(da, k, lane=0):
        source, target, device = (
            (sbp.at[da, 0], rbp.at[da, 0], bm),
            (sbp.at[da, 1], rbp.at[da, 1], bp),
            (sbh.at[da, 0], rbh.at[da, 0], bm),
            (sbh.at[da, 1], rbh.at[da, 1], bp),
        )[k]
        return copy(source, target, kb_r.at[da, k], device, lane)

    def ka_copy(k, lane=0):
        source, target, device = (
            (sap.at[0], rap.at[0], am),
            (sap.at[1], rap.at[1], ap),
            (sah.at[0], rah.at[0], am),
            (sah.at[1], rah.at[1], ap),
        )[k]
        return copy(source, target, ka_r.at[k], device, lane)

    def chip_sum(da, db):
        p = same_index(da, db)
        value = partial(p)
        if db == 2:
            copy(rb.at[da], rb.at[da], kx_r.at[da], sib).wait_recv()
        return [
            only(rsub_ref[0, p] == h, value) + rb[da, db, h].astype(F32) for h in (0, 1)
        ]

    def b_far(da):
        v0, v1 = chip_sum(da, 2)
        sbh[da, 0] = v0.astype(BF)
        start(kb_copy, da, 2)
        sbh[da, 1] = v1.astype(BF)
        start(kb_copy, da, 3)

    def b_near(da, db=None):
        if db != 3:
            b_near_1(da)
        if db != 1:
            b_near_3(da)

    def b_near_1(da):
        v0, v1 = chip_sum(da, 1)
        sbp[da, 0, 1] = v1.astype(BF)
        kb_copy(da, 2).wait_recv()
        sbp[da, 0, 0] = (v0 + rbh[da, 0].astype(F32)).astype(BF)
        start(kb_copy, da, 0)

    def b_near_3(da):
        v0, v1 = chip_sum(da, 3)
        sbp[da, 1, 0] = v0.astype(BF)
        kb_copy(da, 3).wait_recv()
        sbp[da, 1, 1] = (v1 + rbh[da, 1].astype(F32)).astype(BF)
        start(kb_copy, da, 1)

    def row_sum(da):
        v = chip_sum(da, 0)
        kb_copy(da, 0).wait_recv()
        kb_copy(da, 1).wait_recv()
        return [v[h] + rbp[da, 0, h].astype(F32) + rbp[da, 1, h].astype(F32) for h in (0, 1)]

    def a_far():
        v = row_sum(2)
        sah[0] = v[0].astype(BF)
        start(ka_copy, 2)
        sah[1] = v[1].astype(BF)
        start(ka_copy, 3)

    def a_near():
        v = row_sum(1)
        ka_copy(2).wait_recv()
        sap[0, 0] = (v[0] + rah[0].astype(F32)).astype(BF)
        sap[0, 1] = v[1].astype(BF)
        start(ka_copy, 0)
        v = row_sum(3)
        ka_copy(3).wait_recv()
        sap[1, 0] = v[0].astype(BF)
        sap[1, 1] = (v[1] + rah[1].astype(F32)).astype(BF)
        start(ka_copy, 1)

    def add_local(first):
        entries = [REMOTE + first + k for k in range(4)]
        values = [partial(i) for i in entries]
        blocks = [src_ref[0, tab[0, i]] for i in entries]
        for n in range(OWN):
            gself[n] += sum(only(j == n, value) for j, value in zip(blocks, values))

    def add_own():
        value = partial(N_SUB + c)
        for h in (0, 1):
            gself[h] += only(rclu_ref[0, c] == h, value)

    def grad_self():
        gself[...] = dot_nt(grad_pre, ws[...]).reshape(OWN, BLK, D)

    z_partials(HALF)
    k_step(HALF, True)
    z_partials(7)
    k_step(7, False)
    x_send(2)
    x_send(1)
    z_partials(6)
    k_step(7, True)
    x_send(3)
    k_step(6, False)
    x_send(0)
    z_partials(5)
    k_step(6, True)
    b_far(2)
    drain(32)
    k_step(5, False)
    b_far(1)
    z_partials(4)
    k_step(5, True)
    b_far(3)
    b_far(0)
    drain(32)
    k_step(4, False)
    b_near(2)
    z_partials(3)
    k_step(4, True)
    b_near(1)
    drain(32)
    k_step(3, False)
    b_near(3)
    z_partials(2)
    k_step(3, True)
    a_far()
    drain(32)
    k_step(2, False)
    b_near(0)
    z_partials(1)
    k_step(2, True)
    grad_self()
    add_local(0)
    drain(28)
    k_step(1, False)
    a_near()
    add_local(4)
    k_step(1, True)
    add_local(8)
    add_own()
    drain(16)

    v = row_sum(0)
    ka_copy(0).wait_recv()
    ka_copy(1).wait_recv()
    puts = []

    def put(h, rows, k):
        puts.append(pltpu.make_async_copy(out.at[h, rows], out_hbm.at[h, rows], in_s.at[k]))
        puts[-1].start()

    out[2] = gself[2].astype(BF)
    put(2, pl.ds(0, BLK), CHUNKS)
    for q in range(CHUNKS):
        h, rows = rows_of(q)
        total = gself[h, rows] + v[h][q % PER * ROWS : (q % PER + 1) * ROWS]
        total = total + rap[0, h, rows].astype(F32) + rap[1, h, rows].astype(F32)
        for up_way, buf in ((True, ru), (False, rd)):
            k_copy(up_way, 1, q).wait_recv()
            total = total + buf[0, h, rows].astype(F32)
        out[h, rows] = total.astype(BF)
        put(h, rows, q)

    drain(0)
    for cp in puts:
        cp.wait()


def shards(
    features, grad_out, w_self, w_neigh, bias, tile_dst, tile_src, tile_weight, recv_sub, recv_cluster
):
    blk = (BLK, D)
    ring_sems = [(HALF, CHUNKS)] * 2
    sems = [(POOL,)] + ring_sems + [(3,), (RING, 3), (RING,), (CHUNKS,), (4,), (RING, 4), (RING,)]
    scratch = [
        pltpu.VMEM((OWN,) + blk, BF),
        pltpu.SMEM((1, TILES), jnp.int32),
        pltpu.SMEM((1, TILES), jnp.int32),
        pltpu.SMEM((1, N_SUB), jnp.int32),
        pltpu.SMEM((1, NZ), jnp.int32),
        pltpu.VMEM((OWN,) + blk, BF),
        pltpu.VMEM((OWN * BLK, D), BF),
        pltpu.VMEM((D, D), BF),
        pltpu.VMEM((D, D), BF),
        pltpu.VMEM((1, D), F32),
        pltpu.VMEM((1, TILES), jnp.int32),
        pltpu.VMEM((1, SLOTS), jnp.int32),
        pltpu.VMEM((TILES, BLK, BLK), BF),
        pltpu.VMEM((TILES, BLK, BLK), BF),
        pltpu.SMEM((1, SLOTS), jnp.int32),
        pltpu.VMEM((OWN * BLK, D), F32),
        pltpu.VMEM((OWN * BLK, BLK), F32),
        pltpu.VMEM((OWN * BLK, D), F32),
        pltpu.VMEM((OWN * BLK, D), F32),
        pltpu.VMEM((OWN,) + blk, BF),
        pltpu.VMEM((OWN,) + blk, F32),
        pltpu.VMEM((HALF, 2) + blk, BF),
        pltpu.VMEM((HALF, 2) + blk, BF),
        pltpu.VMEM((RING, RING, 2) + blk, BF),
        pltpu.VMEM((RING, RING, 2) + blk, BF),
        pltpu.VMEM((HALF,) + blk, F32),
        pltpu.VMEM((HALF,) + blk, F32),
        pltpu.VMEM((HALF, 2) + blk, BF),
        pltpu.VMEM((HALF, 2) + blk, BF),
        pltpu.VMEM((HALF, 2) + blk, BF),
        pltpu.VMEM((HALF, 2) + blk, BF),
        pltpu.VMEM((RING, RING, 2) + blk, BF),
        pltpu.VMEM((RING, RING, 2) + blk, BF),
        pltpu.VMEM((RING, 2, 2) + blk, BF),
        pltpu.VMEM((RING, 2) + blk, BF),
        pltpu.VMEM((RING, 2, 2) + blk, BF),
        pltpu.VMEM((RING, 2) + blk, BF),
        pltpu.VMEM((2, 2) + blk, BF),
        pltpu.VMEM((2,) + blk, BF),
        pltpu.VMEM((2, 2) + blk, BF),
        pltpu.VMEM((2,) + blk, BF),
        pltpu.SemaphoreType.DMA((12,)),
    ] + [pltpu.SemaphoreType.DMA(shape) for shape in sems]
    result = pl.pallas_call(
        kernel,
        out_shape=jax.ShapeDtypeStruct((OWN,) + blk, BF),
        in_specs=[pl.BlockSpec(memory_space=pl.ANY)] * 10,
        out_specs=pl.BlockSpec(memory_space=pl.ANY),
        scratch_shapes=scratch,
        compiler_params=pltpu.CompilerParams(
            collective_id=0, has_side_effects=True, vmem_limit_bytes=VMEM_BYTES
        ),
        name="sage_layer",
    )(
        tile_src.reshape(1, TILES), tile_dst.reshape(1, TILES), recv_sub, recv_cluster,
        features.reshape((OWN,) + blk), grad_out, w_self, w_neigh, bias.reshape(1, D), tile_weight,
    )
    return result.reshape(OWN * BLK, D)


def solution(mesh):
    rows = P(("cluster", "sub"), None)
    flat = P(("cluster", "sub"))
    placed = (rows, rows, P(), P(), P(), flat, flat, P(("cluster", "sub"), None, None), rows, rows)
    return jax.shard_map(shards, mesh=mesh, in_specs=placed, out_specs=rows, check_vma=False)
```
